128 devices in a mesh: dp: 4 (over z_hi, core), mp: 32 (over y, x, z_lo).
Axes of the slice: x: 4, y: 4, z: 4 (z_hi: 2, z_lo: 2; z = z_hi * 2 + z_lo), core: 2. Of those that a mesh axis runs over, the one named last changes fastest.
Arguments:
- tokens: bfloat16 [2048, 6144], P('dp', 'mp'), may hold values from -6 to 6
- member: int32 [8], P('dp'), may hold values from 0 to 3
- up_weight: bfloat16 [6144, 12288], P('dp', 'mp'), may hold values from -0.078125 to 0.078125
- down_weight: bfloat16 [6144, 12288], P('dp', 'mp'), may hold values from -0.0546875 to 0.0546875
- in_fast: bfloat16 [4, 6144], P(None, 'mp'), may hold values from 0.099609375 to 1.8984375
- hidden_fast: bfloat16 [4, 12288], P(None, 'mp'), may hold values from 0.099609375 to 1.8984375
- mid_fast: bfloat16 [4, 12288], P(None, 'mp'), may hold values from 0.099609375 to 1.8984375
- out_fast: bfloat16 [4, 6144], P(None, 'mp'), may hold values from 0.099609375 to 1.8984375
- cotangent: bfloat16 [2048, 6144], P('dp', 'mp'), may hold values from -0.3125 to 0.3125
Outputs:
- layer_out: bfloat16 [2048, 6144], P('dp', 'mp')
- up_grad: float32 [6144, 12288], P('dp', 'mp')
- down_grad: float32 [6144, 12288], P('dp', 'mp')
- in_fast_grad: float32 [4, 6144], P(None, 'mp')
- hidden_fast_grad: float32 [4, 12288], P(None, 'mp')
- mid_fast_grad: float32 [4, 12288], P(None, 'mp')
- out_fast_grad: float32 [4, 6144], P(None, 'mp')
The draws below stay inside these ranges and needn't reach their ends.
All inputs are finite; a program needn't handle non-finite values.
Results may differ from the reference program's by a relative error of at most 0.03.
Values may be sent and summed in bfloat16 or wider, within the bound.
A program may use at most 128 MiB of HBM per device.

```python
import math
import jax
import jax.numpy as jnp
from jax import lax

D = 6144
FF = 12288
MEMBERS = 4
PATCHES = 256
TOK_DEV = 512
IMAGES = 8
TOKENS = 2048
N_DP = 4
N_MP = 32


def set_ends(values, own_key, low, largest):
    shape = values.shape
    index_at = [jax.random.randint(jax.random.fold_in(own_key, axis), (), 0, shape[axis]) for axis in range(len(shape))]
    values = values.at[tuple(index_at)].set(low)
    longest = shape.index(max(shape))
    index_at[longest] = (index_at[longest] + 1) % shape[longest]
    return values.at[tuple(index_at)].set(largest)


def block_levels(own_key, dims, split, low, top_value):
    factor_of = 1.0
    for dim, blocks in split:
        heights = jax.random.uniform(jax.random.fold_in(jax.random.fold_in(own_key, 6), dim), (blocks,), jnp.float32, low / len(split), top_value / len(split))
        factor_of = factor_of * jnp.repeat(jnp.exp(heights), dims[dim] // blocks).reshape((-1,) + (1,) * (len(dims) - 1 - dim))
    return factor_of


def centred(stream_key, shape, width, reach, pieces=(), held_as=jnp.bfloat16):
    array = jax.random.normal(stream_key, shape, jnp.float32) * width
    if len(pieces) > 0:
        array = block_levels(stream_key, shape, pieces, -0.22, 0.18) * array
    return jnp.clip(array, min=-reach, max=reach).astype(held_as)


def setup_inputs(seed: int = 0) -> dict:
    arg_keys = jax.random.split(jax.random.key(seed), 10)
    return {
        "tokens": centred(arg_keys[0], (TOKENS, D), 1.0, 6.0, ((0, 4), (1, 32))),
        "member": set_ends(jax.random.randint(arg_keys[1], (IMAGES,), 0, MEMBERS), jax.random.fold_in(arg_keys[1], 1), 0, MEMBERS - 1).astype(jnp.int32),
        "up_weight": centred(arg_keys[2], (D, FF), D ** -0.5, 0.078125, ((0, 4), (1, 32))),
        "down_weight": centred(arg_keys[3], (D, FF), FF ** -0.5, 0.0546875, ((0, 4), (1, 32))),
        "in_fast": jnp.clip(1.0 + 0.18 * jax.random.normal(arg_keys[4], (MEMBERS, D), jnp.float32), 0.099609375, 1.8984375).astype(jnp.bfloat16),
        "hidden_fast": jnp.clip(1.0 + 0.18 * jax.random.normal(arg_keys[5], (MEMBERS, FF), jnp.float32), 0.099609375, 1.8984375).astype(jnp.bfloat16),
        "mid_fast": jnp.clip(1.0 + 0.18 * jax.random.normal(arg_keys[6], (MEMBERS, FF), jnp.float32), 0.099609375, 1.8984375).astype(jnp.bfloat16),
        "out_fast": jnp.clip(1.0 + 0.18 * jax.random.normal(arg_keys[7], (MEMBERS, D), jnp.float32), 0.099609375, 1.8984375).astype(jnp.bfloat16),
        "cotangent": centred(arg_keys[8], (TOKENS, D), (TOKENS ** -0.5), 0.3125, ((0, 4), (1, 32))),
    }


gelu_scale = math.sqrt(2.0 / math.pi)

def gelu_parts(gated):
    tanh_arg = gelu_scale * (gated + 0.044715 * gated * gated * gated)
    tangent = jnp.tanh(tanh_arg)
    result_value = 0.5 * gated * (1.0 + tangent)
    derivative = 0.5 * (1.0 + tangent) + 0.5 * gated * (1.0 - tangent * tangent) * gelu_scale * (1.0 + 3.0 * 0.044715 * gated * gated)
    return (result_value, derivative)

def reference(tokens, member, up_weight, down_weight, in_fast, hidden_fast, mid_fast, out_fast, cotangent):
    tok_member = jnp.repeat(member, PATCHES).astype(jnp.int32)
    selector = (tok_member[:, None] == jnp.arange(MEMBERS, dtype=jnp.int32)[None, :]).astype(jnp.float32)

    def per_member(values):
        return jnp.dot(selector.T, values, precision=lax.Precision.HIGHEST)
    tok_float = tokens.astype(jnp.float32)
    average = lax.optimization_barrier(jnp.mean(tok_float, axis=-1, keepdims=True))
    centered = tok_float - average
    variance = lax.optimization_barrier(jnp.mean(centered * centered, axis=-1, keepdims=True))
    normed = centered * lax.rsqrt(variance + 1e-06)
    layer_in = (normed * in_fast.astype(jnp.float32)[tok_member]).astype(jnp.bfloat16)
    pre_act = jnp.dot(layer_in, up_weight, preferred_element_type=jnp.float32)
    hid_row = hidden_fast.astype(jnp.float32)[tok_member]
    mid_row = mid_fast.astype(jnp.float32)[tok_member]
    out_row = out_fast.astype(jnp.float32)[tok_member]
    gated = pre_act * hid_row
    activated, derivative = gelu_parts(gated)
    hidden = (activated * mid_row).astype(jnp.bfloat16)
    block_width = FF // N_MP
    hidden_blocks = hidden.reshape(TOKENS, N_MP, block_width).transpose(1, 0, 2)
    down_blocks = down_weight.reshape(D, N_MP, block_width).transpose(1, 0, 2)

    def add_block(running, operands):
        hid_part, down_part = operands
        partial_sum = lax.dot_general(hid_part, down_part, (((1,), (1,)), ((), ())), preferred_element_type=jnp.float32)
        rounded = lax.optimization_barrier(partial_sum.astype(jnp.bfloat16))
        return (running + rounded.astype(jnp.float32), None)
    branch = lax.scan(add_block, jnp.zeros((TOKENS, D), jnp.float32), (hidden_blocks, down_blocks))[0]
    layer_out = (tok_float + branch * out_row).astype(jnp.bfloat16)
    cot_float = cotangent.astype(jnp.float32)
    down_cot = (cot_float * out_row).astype(jnp.bfloat16)
    out_fast_grad = per_member(cot_float * branch)
    grad_act = jnp.dot(down_cot, down_weight, preferred_element_type=jnp.float32)
    mid_fast_grad = per_member(activated * grad_act)
    grad_gated = grad_act * mid_row * derivative
    hidden_fast_grad = per_member(pre_act * grad_gated)
    up_cot = (grad_gated * hid_row).astype(jnp.bfloat16)
    grouped = (layer_in.reshape(N_DP, TOK_DEV, D), up_cot.reshape(N_DP, TOK_DEV, FF), down_cot.reshape(N_DP, TOK_DEV, D), hidden.reshape(N_DP, TOK_DEV, FF))

    def add_group(running, operands):
        in_part, up_part, down_part, hid_part = operands
        up_term = lax.dot_general(in_part, up_part, (((0,), (0,)), ((), ())), preferred_element_type=jnp.float32)
        down_term = lax.dot_general(down_part, hid_part, (((0,), (0,)), ((), ())), preferred_element_type=jnp.float32)
        up_round = lax.optimization_barrier(up_term.astype(jnp.bfloat16))
        down_round = lax.optimization_barrier(down_term.astype(jnp.bfloat16))
        return ((running[0] + up_round.astype(jnp.float32), running[1] + down_round.astype(jnp.float32)), None)
    zero_grad = jnp.zeros((D, FF), jnp.float32)
    up_grad, down_grad = lax.scan(add_group, (zero_grad, zero_grad), grouped)[0]
    projected = lax.dot_general(up_cot, up_weight, (((1,), (1,)), ((), ())), preferred_element_type=jnp.float32)
    in_fast_grad = per_member(normed * projected)
    return (layer_out, up_grad, down_grad, in_fast_grad, hidden_fast_grad, mid_fast_grad, out_fast_grad)
```

```python
import math

import jax
import jax.numpy as jnp
from jax import lax
from jax.experimental import pallas as pl
from jax.experimental.pallas import tpu as pltpu
from jax.sharding import Mesh
from jax.sharding import PartitionSpec as P

AXES = ("h", "c", "y", "x", "l")
SIZES = dict(h=2, c=2, y=4, x=4, l=2)
MESH = pl.DeviceIdType.MESH
F32 = jnp.float32
BF16 = jnp.bfloat16
gelu_scale = math.sqrt(2.0 / math.pi)

D_BLK = 1536
PIECE = 192
PAIR = 384
IMG = 256
N_IMG = 8
FFB = 384
HALF = 192
N_SEM = 240


def dot(a, b):
    return jnp.dot(a, b, preferred_element_type=F32)


def dot_t(a, b):
    return lax.dot_general(a, b, (((1,), (1,)), ((), ())), preferred_element_type=F32)


def gelu_parts(gated):
    tanh_arg = gelu_scale * (gated + 0.044715 * gated * gated * gated)
    tangent = jnp.tanh(tanh_arg)
    result_value = 0.5 * gated * (1.0 + tangent)
    derivative = 0.5 * (1.0 + tangent) + 0.5 * gated * (1.0 - tangent * tangent) * gelu_scale * (
        1.0 + 3.0 * 0.044715 * gated * gated
    )
    return (result_value, derivative)


def kernel(
    xt, ct, tab, sel_own, wu, wd, hf, mf,
    bo, ug, dg, fin_in, fin_out, fin_mh,
    gx, xn, gc, wut, wdt, eye, tabs, tabt, sel, stats,
    pa, p_send, p_recv, h_send, h_recv, hid, upc, cot_own,
    rf, rv, ruf, ru, rl, fb, bo_in,
    in_acc, in_recv, y_in, y_out, s_send, s_recv, mh_own, mh_all, ss, rs,
):
    h, c, y, x, l = [lax.axis_index(a) for a in AXES]
    here = dict(h=h, c=c, y=y, x=x, l=l)
    dp = 2 * h + c

    def at(**off):
        pos = dict(here)
        for axis, step in off.items():
            pos[axis] = lax.rem(pos[axis] + (step + SIZES[axis]), SIZES[axis])
        return tuple(pos[a] for a in AXES)

    partner = (y // 2, lax.rem(y, 2), dp, x, l)
    is_self = y == dp
    dp_parts = [at(c=1), at(h=1), at(h=1, c=1)]
    xl_parts = [(dx, dl) for dx in (0, 1, 2, 3) for dl in (0, 1) if dx or dl]
    y_parts = [1, 2, 3]

    counter = [0]
    sends = []

    def start(src, dst, dev):
        i = counter[0]
        counter[0] += 1
        copy = pltpu.make_async_remote_copy(
            src_ref=src, dst_ref=dst, send_sem=ss.at[i], recv_sem=rs.at[i],
            device_id=dev, device_id_type=MESH,
        )
        copy.start()
        sends.append(copy.wait_send)
        return copy

    def start_swap(src, dst):
        i = counter[0]
        counter[0] += 1
        copy = pltpu.make_async_remote_copy(
            src_ref=src, dst_ref=dst, send_sem=ss.at[i], recv_sem=rs.at[i],
            device_id=partner, device_id_type=MESH,
        )

        @pl.when(jnp.logical_not(is_self))
        def _():
            copy.start()

        @pl.when(is_self)
        def _():
            pltpu.make_async_copy(src, dst, rs.at[i]).start()

        def wait_send():
            @pl.when(jnp.logical_not(is_self))
            def _():
                copy.wait_send()

        sends.append(wait_send)
        return copy

    def drain():
        for wait in sends:
            wait()
        sends.clear()

    bar = pltpu.get_barrier_semaphore()
    greet = dp_parts + [at(x=dx, l=dl) for dx, dl in xl_parts] + [at(y=dy) for dy in y_parts]
    for dev in greet:
        pl.semaphore_signal(bar, inc=1, device_id=dev, device_id_type=MESH)

    @pl.when(jnp.logical_not(is_self))
    def _():
        pl.semaphore_signal(bar, inc=1, device_id=partner, device_id_type=MESH)

    pl.semaphore_wait(bar, jnp.where(is_self, len(greet), len(greet) + 1))

    own_piece = 2 * x + l
    own_rows = pl.ds(pl.multiple_of(PIECE * own_piece, PIECE), PIECE)

    swap_x = [start_swap(xt.at[j], gx.at[2 * dp + j, own_rows]) for j in (0, 1)]
    swap_tab = start_swap(tab, tabs.at[own_piece])
    sel_mine = sel.at[pl.ds(2 * dp, 2)]
    sel[pl.ds(2 * dp, 2)] = sel_own[...]
    sel_copies = [start(sel_own, sel_mine, dev) for dev in dp_parts]
    swap_c = [start_swap(ct.at[j], gc.at[2 * dp + j, own_rows]) for j in (0, 1)]

    def chunk(ref, j, du, dv, q=None):
        dy, dx = (dv, du) if j == 0 else (du, dv)
        img = 2 * lax.rem(y + (dy + 4), 4) + j
        row = PAIR * lax.rem(x + (dx + 4), 4)
        size = PAIR
        if q is not None:
            row, size = row + PIECE * q, PIECE
        return ref.at[img, pl.ds(pl.multiple_of(row, PIECE), size)]

    def u_dev(j, step):
        return at(x=step) if j == 0 else at(y=step)

    def v_dev(j, step):
        return at(y=step) if j == 0 else at(x=step)

    def gather(buf, swaps):
        both = (0, 1)
        r = [dict(), dict()]

        def u_send(j, du, q, step, name):
            piece = chunk(buf, j, du, 0, q)
            r[j][name] = start(piece, piece, u_dev(j, step))

        def v_send(j, du, dv, step, name):
            part = chunk(buf, j, du, dv)
            r[j][name] = start(part, part, v_dev(j, step))

        for j in both:
            swaps[j].wait_recv()
            piece = chunk(buf, j, 0, 0, l)
            r[j]["l"] = start(piece, piece, at(l=1))
            u_send(j, 0, l, 1, "-own")
            u_send(j, 0, l, -1, "+own")
        yield
        for j in both:
            r[j]["l"].wait_recv()
            u_send(j, 0, 1 - l, 1, "-oth")
            u_send(j, 0, 1 - l, -1, "+oth")
        for j in both:
            r[j]["-own"].wait_recv()
            u_send(j, -1, l, 1, "fwd-")
        for j in both:
            v_send(j, 0, 0, 1, "v-0")
            v_send(j, 0, 0, -1, "v+0")
        yield
        for j in both:
            r[j]["+own"].wait_recv()
            r[j]["+oth"].wait_recv()
            u_send(j, 1, 1 - l, -1, "fwd+")
            v_send(j, 1, 0, 1, "v-1")
            v_send(j, 1, 0, -1, "v+1")
            r[j]["-oth"].wait_recv()
            v_send(j, -1, 0, 1, "v-m")
            v_send(j, -1, 0, -1, "v+m")
        yield
        for j in both:
            r[j]["fwd-"].wait_recv()
            r[j]["fwd+"].wait_recv()
            v_send(j, 2, 0, 1, "v-2")
            v_send(j, 2, 0, -1, "v+2")
        yield
        for j in both:
            r[j]["v-0"].wait_recv()
            v_send(j, 0, -1, 1, "w-0")
            r[j]["v+1"].wait_recv()
            v_send(j, 1, 1, -1, "w+1")
        yield
        for j in both:
            r[j]["v-m"].wait_recv()
            v_send(j, -1, -1, 1, "w-m")
            r[j]["v+2"].wait_recv()
            v_send(j, 2, 1, -1, "w+2")
        yield
        for name in ("v+0", "v+m", "v-1", "v-2", "w-0", "w+1", "w-m", "w+2"):
            for j in both:
                r[j][name].wait_recv()
        yield

    def run(gen, steps=1000):
        for _ in range(steps):
            if next(gen, "end") == "end":
                return

    run_x = gather(gx, swap_x)
    run_c = gather(gc, swap_c)
    run(run_x, 1)

    swap_tab.wait_recv()
    tab_copies = [
        start(tabs.at[own_piece], tabs.at[own_piece], at(x=dx, l=dl)) for dx, dl in xl_parts
    ]
    run(run_x, 1)
    ident = lax.broadcasted_iota(jnp.int32, (FFB, FFB), 0) == lax.broadcasted_iota(
        jnp.int32, (FFB, FFB), 1
    )
    eye[...] = jnp.where(ident, 1.0, 0.0).astype(BF16)
    run(run_x, 1)
    for src, dst in ((wu, wut), (wd, wdt)):
        for k in range(4):
            dst[:, k * 384 : (k + 1) * 384] = dot_t(
                eye[...], src[k * 384 : (k + 1) * 384, :]
            ).astype(BF16)
    run(run_x, 1)
    for copy in tab_copies:
        copy.wait_recv()
    for copy in sel_copies:
        copy.wait_recv()
    for p in range(8):
        tabt[p * PIECE : (p + 1) * PIECE, :] = dot_t(eye[:PIECE, :IMG], tabs[p]).astype(BF16)
    run(run_x)

    order = [
        2 * lax.rem(y + dy, 4) + j for j, dy in
        ((0, 0), (0, 1), (0, 3), (0, 2), (1, 0), (1, 1), (1, 3), (1, 2))
    ]

    def image_stats(img):
        def total(p, acc):
            rows = pl.ds(pl.multiple_of(p * PIECE, PIECE), PIECE)
            v = gx[img, rows].astype(F32).reshape(PIECE // 8, 8, IMG)
            return acc + jnp.sum(v, axis=0)

        def spread(p, acc):
            rows = pl.ds(pl.multiple_of(p * PIECE, PIECE), PIECE)
            v = (gx[img, rows].astype(F32) - mean).reshape(PIECE // 8, 8, IMG)
            return acc + jnp.sum(v * v, axis=0)

        zero = jnp.zeros((8, IMG), F32)
        mean = jnp.sum(lax.fori_loop(0, 8, total, zero), axis=0, keepdims=True) / D_BLK
        dev2 = jnp.sum(lax.fori_loop(0, 8, spread, zero), axis=0, keepdims=True)
        row = lax.broadcasted_iota(jnp.int32, (8, IMG), 0)
        stats[dp, img] = jnp.where(row == 0, mean, jnp.where(row == 1, dev2, 0.0))

    run(run_c, 1)
    for img in order:
        image_stats(img)
    run(run_c, 1)
    stat_copies = [start(stats.at[dp], stats.at[dp], dev) for dev in dp_parts]
    run(run_c, 1)
    for copy in stat_copies:
        copy.wait_recv()

    def normalise(img):
        parts = [stats[k, img] for k in range(4)]
        mean = (parts[0][0:1] + parts[1][0:1] + parts[2][0:1] + parts[3][0:1]) * 0.25
        dev2 = parts[0][1:2] + parts[1][1:2] + parts[2][1:2] + parts[3][1:2]
        for k in range(4):
            gap = parts[k][0:1] - mean
            dev2 = dev2 + D_BLK * (gap * gap)
        rstd = lax.rsqrt(dev2 / (4 * D_BLK) + 1e-06)

        def step(p, carry):
            rows = pl.ds(pl.multiple_of(p * PIECE, PIECE), PIECE)
            factor = dot(tabt[rows, :], sel[img, 0])
            v = (gx[img, rows].astype(F32) - mean) * rstd
            xn[img, rows] = (v * factor).astype(BF16)
            return carry

        lax.fori_loop(0, 8, step, 0)

    mine = pl.ds(pl.multiple_of(HALF * c, HALF), HALF)
    other = pl.ds(pl.multiple_of(HALF * (1 - c), HALF), HALF)
    core = at(c=1)
    far = at(h=1)

    def partial_product(m, weight_t, operand, img):
        p_send[m, img] = dot(weight_t[other, :], operand[img]).astype(BF16)
        copy = start(p_send.at[m, img], p_recv.at[m, img], core)
        pa[m, img] = dot(weight_t[mine, :], operand[img])
        return copy

    def to_far(m, copy, img):
        copy.wait_recv()
        both = pa[m, img] + p_recv[m, img].astype(F32)
        pa[m, img] = both
        h_send[m, img] = both.astype(BF16)
        return start(h_send.at[m, img], h_recv.at[m, img], far)

    hid_copies = []

    def finish_hidden(copy, img):
        copy.wait_recv()
        pre_act = pa[0, img] + h_recv[0, img].astype(F32)
        pa[0, img] = pre_act
        hid_row = dot(hf[mine, :], sel[img, 0])
        mid_row = dot(mf[mine, :], sel[img, 0])
        activated, _ = gelu_parts(pre_act * hid_row)
        hid[img, mine] = (activated * mid_row).astype(BF16)
        hid_copies.append(start(hid.at[img, mine], hid.at[img, mine], core))

    near, wide = [], []
    for n, img in enumerate(order):
        normalise(img)
        near.append(partial_product(0, wut, xn, img))
        if n >= 1:
            wide.append(to_far(0, near[n - 1], order[n - 1]))
        if n % 2 == 1:
            run(run_c, 1)
    wide.append(to_far(0, near[7], order[7]))
    for n, img in enumerate(order):
        finish_hidden(wide[n], img)
    run(run_c)
    drain()

    br = gx
    for n, img in enumerate(order):
        hid_copies[n].wait_recv()

        def rows_of(k, carry, img=img):
            rows = pl.ds(pl.multiple_of(k * PAIR, PAIR), PAIR)
            br[img, rows] = dot(wd[rows, :], hid[img]).astype(BF16)
            return carry

        lax.fori_loop(0, 4, rows_of, 0)

    cot_own[...] = gc[pl.ds(2 * y, 2), own_rows]

    up, down = (0, -1), (1, 2)
    slot = {0: 0, -1: 1, 1: 2, 2: 3}

    def add_into(dst, *terms):
        total = dst[...].astype(F32)
        for term in terms:
            total = total + term[...].astype(F32)
        dst[...] = total.astype(BF16)

    finals = []

    def scatter():
        both = (0, 1)
        r = [dict(), dict()]
        for j in both:
            for i in (0, 1):
                r[j]["f+", up[i]] = start(chunk(br, j, up[i], 2), rf.at[j, 0, i], v_dev(j, 1))
                r[j]["f-", down[i]] = start(chunk(br, j, down[i], 2), rf.at[j, 1, i], v_dev(j, -1))
        for j in both:
            for k in down:
                r[j]["d+", k] = start(chunk(br, j, k, 1), rv.at[j, 0, slot[k]], v_dev(j, 1))
            for k in up:
                r[j]["d-", k] = start(chunk(br, j, k, -1), rv.at[j, 1, slot[k]], v_dev(j, -1))
        yield
        for i in (0, 1):
            for j in both:
                r[j]["f+", up[i]].wait_recv()
                part = chunk(br, j, up[i], 1)
                add_into(part, rf.at[j, 0, i])
                r[j]["d+", up[i]] = start(part, rv.at[j, 0, slot[up[i]]], v_dev(j, 1))
                r[j]["f-", down[i]].wait_recv()
                part = chunk(br, j, down[i], -1)
                add_into(part, rf.at[j, 1, i])
                r[j]["d-", down[i]] = start(part, rv.at[j, 1, slot[down[i]]], v_dev(j, -1))
            yield

        def total(j, k):
            r[j]["d+", k].wait_recv()
            r[j]["d-", k].wait_recv()
            part = chunk(br, j, k, 0)
            add_into(part, rv.at[j, 0, slot[k]], rv.at[j, 1, slot[k]])

        for j in both:
            total(j, 2)
            r[j]["uf+"] = start(chunk(br, j, 2, 0, 0), ruf.at[j, 0], u_dev(j, 1))
            r[j]["uf-"] = start(chunk(br, j, 2, 0, 1), ruf.at[j, 1], u_dev(j, -1))
        yield
        lo, hi = pl.ds(0, PIECE), pl.ds(PIECE, PIECE)
        for j in both:
            total(j, 1)
            r[j]["u+1"] = start(chunk(br, j, 1, 0, 1), ru.at[j, 0, hi], u_dev(j, 1))
            total(j, -1)
            r[j]["u-0"] = start(chunk(br, j, -1, 0, 0), ru.at[j, 1, lo], u_dev(j, -1))
        yield
        for j in both:
            r[j]["uf+"].wait_recv()
            part = chunk(br, j, 1, 0, 0)
            add_into(part, ruf.at[j, 0])
            r[j]["u+0"] = start(part, ru.at[j, 0, lo], u_dev(j, 1))
            r[j]["uf-"].wait_recv()
            part = chunk(br, j, -1, 0, 1)
            add_into(part, ruf.at[j, 1])
            r[j]["u-1"] = start(part, ru.at[j, 1, hi], u_dev(j, -1))
        for j in both:
            total(j, 0)
        yield
        for j in both:
            for name in ("u+1", "u+0", "u-0", "u-1"):
                r[j][name].wait_recv()
            add_into(chunk(br, j, 0, 0), ru.at[j, 0], ru.at[j, 1])
            r[j]["l"] = start(chunk(br, j, 0, 0, 1 - l), rl.at[j], at(l=1))
        yield
        for j in both:
            r[j]["l"].wait_recv()
            total_piece = chunk(br, j, 0, 0, l)[...].astype(F32) + rl[j].astype(F32)
            fb[j] = total_piece.astype(BF16)
            finals.append(start_swap(fb.at[j], bo_in.at[j]))
        yield

    run_s = scatter()
    run(run_s, 1)

    def scale_cot(img):
        def step(p, carry):
            rows = pl.ds(pl.multiple_of(p * PIECE, PIECE), PIECE)
            factor = dot(tabt[rows, :], sel[img, 1])
            gc[img, rows] = (gc[img, rows].astype(F32) * factor).astype(BF16)
            return carry

        lax.fori_loop(0, 8, step, 0)

    near, wide = [], []
    for n, img in enumerate(order):
        scale_cot(img)
        near.append(partial_product(1, wdt, gc, img))
        if n >= 1:
            wide.append(to_far(1, near[n - 1], order[n - 1]))
    wide.append(to_far(1, near[7], order[7]))
    run(run_s, 1)

    def down_rows(k, carry):
        rows = pl.ds(pl.multiple_of(k * PAIR, PAIR), PAIR)
        acc = dot_t(gc[0, rows], hid[0])
        for img in range(1, 8):
            acc = acc + dot_t(gc[img, rows], hid[img])
        dg[rows, :] = acc
        return carry

    lax.fori_loop(0, 4, down_rows, 0)
    run(run_s, 1)

    mh_own[...] = jnp.zeros((32, IMG), F32)
    upc_copies = []
    for n, img in enumerate(order):
        wide[n].wait_recv()
        grad_act = pa[1, img] + h_recv[1, img].astype(F32)
        pre_act = pa[0, img]
        hid_row = dot(hf[mine, :], sel[img, 0])
        mid_row = dot(mf[mine, :], sel[img, 0])
        activated, derivative = gelu_parts(pre_act * hid_row)
        grad_gated = grad_act * mid_row * derivative
        upc[img, mine] = (grad_gated * hid_row).astype(BF16)
        upc_copies.append(start(upc.at[img, mine], upc.at[img, mine], core))
        pick = sel[img, 0]
        mh_own[0:16, 0:HALF] += dot_t(pick, (activated * grad_act).astype(BF16))
        mh_own[16:32, 0:HALF] += dot_t(pick, (pre_act * grad_gated).astype(BF16))
    mh_all[dp] = mh_own[...]
    mh_copies = [start(mh_own, mh_all.at[dp], dev) for dev in dp_parts]
    run(run_s, 1)
    for copy in upc_copies:
        copy.wait_recv()

    in_acc[...] = jnp.zeros((8, 16, IMG), F32)
    for n, img in enumerate(order):
        def in_rows(p, carry, img=img):
            rows = pl.ds(pl.multiple_of(p * PIECE, PIECE), PIECE)
            prod = dot(wu[rows, :], upc[img]) * xn[img, rows].astype(F32)
            in_acc[p, :, 0:PIECE] += dot_t(sel[img, 0], prod.astype(BF16))
            return carry

        lax.fori_loop(0, 8, in_rows, 0)
    in_copies = []
    for i, (dx, dl) in enumerate(xl_parts):
        p_to = 2 * lax.rem(x + dx, 4) + lax.rem(l + dl, 2)
        in_copies.append(start(in_acc.at[p_to], in_recv.at[i], at(x=dx, l=dl)))
    run(run_s, 1)

    def up_rows(k, carry):
        rows = pl.ds(pl.multiple_of(k * PAIR, PAIR), PAIR)
        acc = dot_t(xn[0, rows], upc[0])
        for img in range(1, 8):
            acc = acc + dot_t(xn[img, rows], upc[img])
        ug[rows, :] = acc
        return carry

    lax.fori_loop(0, 4, up_rows, 0)
    run(run_s, 1)

    for copy in in_copies:
        copy.wait_recv()
    total_in = in_acc[own_piece]
    for i in range(7):
        total_in = total_in + in_recv[i]
    y_in[y] = total_in
    y_in_copies = [start(y_in.at[y], y_in.at[y], at(y=dy)) for dy in y_parts]
    run(run_s)

    out_total = jnp.zeros((16, PIECE), F32)
    for j in (0, 1):
        prod = cot_own[j].astype(F32) * fb[j].astype(F32)
        out_total = out_total + dot_t(sel[2 * y + j, 0], prod.astype(BF16))
    y_out[y] = jnp.zeros((16, IMG), F32)
    y_out[y, :, 0:PIECE] = out_total
    y_out_copies = [start(y_out.at[y], y_out.at[y], at(y=dy)) for dy in y_parts]
    for copy in y_in_copies + y_out_copies:
        copy.wait_recv()
    s_send[0] = (y_in[0] + y_in[1]) + (y_in[2] + y_in[3])
    s_send[1] = (y_out[0] + y_out[1]) + (y_out[2] + y_out[3])
    last = start_swap(s_send, s_recv)
    for copy in mh_copies:
        copy.wait_recv()
    fin_mh[...] = mh_all[...]
    for copy in finals:
        copy.wait_recv()
    bo[...] = bo_in[...]
    last.wait_recv()
    fin_in[...] = s_recv[0]
    fin_out[...] = s_recv[1]
    drain()


def exchange(xt, ct, tab, sel_own, wu, wd, hf, mf):
    vmem = pl.BlockSpec(memory_space=pltpu.VMEM)
    out_shape = [
        jax.ShapeDtypeStruct((2, PIECE, IMG), BF16),
        jax.ShapeDtypeStruct((D_BLK, FFB), F32),
        jax.ShapeDtypeStruct((D_BLK, FFB), F32),
        jax.ShapeDtypeStruct((16, IMG), F32),
        jax.ShapeDtypeStruct((16, IMG), F32),
        jax.ShapeDtypeStruct((4, 32, IMG), F32),
    ]
    scratch = [
        ((N_IMG, D_BLK, IMG), BF16),
        ((N_IMG, D_BLK, IMG), BF16),
        ((N_IMG, D_BLK, IMG), BF16),
        ((FFB, D_BLK), BF16),
        ((FFB, D_BLK), BF16),
        ((FFB, FFB), BF16),
        ((8, 16, IMG), BF16),
        ((D_BLK, 16), BF16),
        ((N_IMG, 2, 16, IMG), BF16),
        ((4, N_IMG, 8, IMG), F32),
        ((2, N_IMG, HALF, IMG), F32),
        ((2, N_IMG, HALF, IMG), BF16),
        ((2, N_IMG, HALF, IMG), BF16),
        ((2, N_IMG, HALF, IMG), BF16),
        ((2, N_IMG, HALF, IMG), BF16),
        ((N_IMG, FFB, IMG), BF16),
        ((N_IMG, FFB, IMG), BF16),
        ((2, PIECE, IMG), BF16),
        ((2, 2, 2, PAIR, IMG), BF16),
        ((2, 2, 4, PAIR, IMG), BF16),
        ((2, 2, PIECE, IMG), BF16),
        ((2, 2, PAIR, IMG), BF16),
        ((2, PIECE, IMG), BF16),
        ((2, PIECE, IMG), BF16),
        ((2, PIECE, IMG), BF16),
        ((8, 16, IMG), F32),
        ((7, 16, IMG), F32),
        ((4, 16, IMG), F32),
        ((4, 16, IMG), F32),
        ((2, 16, IMG), F32),
        ((2, 16, IMG), F32),
        ((32, IMG), F32),
        ((4, 32, IMG), F32),
    ]
    return pl.pallas_call(
        kernel,
        out_shape=out_shape,
        in_specs=[vmem] * 8,
        out_specs=[vmem] * 6,
        scratch_shapes=[pltpu.VMEM(s, d) for s, d in scratch]
        + [pltpu.SemaphoreType.DMA((N_SEM,)), pltpu.SemaphoreType.DMA((N_SEM,))],
        compiler_params=pltpu.CompilerParams(
            collective_id=0, has_side_effects=True, vmem_limit_bytes=62 * 1024 * 1024
        ),
        cost_estimate=pl.CostEstimate(
            flops=14_500_000_000, bytes_accessed=12_000_000, transcendentals=1_600_000
        ),
    )(xt, ct, tab, sel_own, wu, wd, hf, mf)


def body(
    tokens, member, up_weight, down_weight, in_fast, hidden_fast, mid_fast, out_fast, cotangent
):
    def by_image(a):
        return a.reshape(2, IMG, PIECE).transpose(0, 2, 1)

    zero4 = jnp.zeros((4, PIECE), BF16)
    tab = jnp.pad(
        jnp.concatenate([in_fast, out_fast, zero4, zero4], axis=0), ((0, 0), (0, IMG - PIECE))
    )
    row = jnp.arange(16, dtype=jnp.int32)[None, None, :, None]
    shift = jnp.array([0, 4], jnp.int32)[None, :, None, None]
    sel_own = jnp.broadcast_to(
        (row == member[:, None, None, None] + shift).astype(BF16), (2, 2, 16, IMG)
    )
    hf = jnp.pad(hidden_fast.T, ((0, 0), (0, 12)))
    mf = jnp.pad(mid_fast.T, ((0, 0), (0, 12)))
    branch, ug, dg, fin_in, fin_out, fin_mh = exchange(
        by_image(tokens), by_image(cotangent), tab, sel_own, up_weight, down_weight, hf, mf
    )
    out_rows = jnp.repeat(out_fast.astype(F32)[member], IMG, axis=0)
    branch = branch.transpose(0, 2, 1).reshape(2 * IMG, PIECE).astype(F32)
    layer_out = (tokens.astype(F32) + branch * out_rows).astype(BF16)
    in_grad = fin_in[0:4, 0:PIECE] / in_fast.astype(F32)
    out_grad = fin_out[0:4, 0:PIECE]
    mid_grad = jnp.concatenate([fin_mh[0, 0:4, 0:HALF], fin_mh[1, 0:4, 0:HALF]], axis=1)
    hidden_grad = jnp.concatenate([fin_mh[0, 16:20, 0:HALF], fin_mh[1, 16:20, 0:HALF]], axis=1)
    return (layer_out, ug, dg, in_grad, hidden_grad, mid_grad, out_grad)


def solution(mesh):
    grid = Mesh(mesh.devices.reshape([SIZES[a] for a in AXES]), AXES)
    dp, mp = ("h", "c"), ("y", "x", "l")
    in_specs = (
        P(dp, mp),
        P(dp),
        P(dp, mp),
        P(dp, mp),
        P(None, mp),
        P(None, mp),
        P(None, mp),
        P(None, mp),
        P(dp, mp),
    )
    out_specs = (
        P(dp, mp),
        P(dp, mp),
        P(dp, mp),
        P(None, mp),
        P(None, mp),
        P(None, mp),
        P(None, mp),
    )
    return jax.shard_map(body, mesh=grid, in_specs=in_specs, out_specs=out_specs, check_vma=False)
```

```python
import math

import jax
import jax.numpy as jnp
from jax import lax
from jax.experimental import pallas as pl
from jax.experimental.pallas import tpu as pltpu
from jax.sharding import Mesh
from jax.sharding import PartitionSpec as P

AXES = ("h", "c", "y", "x", "l")
SIZES = dict(h=2, c=2, y=4, x=4, l=2)
MESH = pl.DeviceIdType.MESH
F32 = jnp.float32
BF16 = jnp.bfloat16
gelu_scale = math.sqrt(2.0 / math.pi)

D_BLK = 1536
PIECE = 192
PAIR = 384
IMG = 256
N_IMG = 8
FFB = 384
HALF = 192
N_SEM = 240


def dot(a, b):
    return jnp.dot(a, b, preferred_element_type=F32)


def dot_t(a, b):
    return lax.dot_general(a, b, (((1,), (1,)), ((), ())), preferred_element_type=F32)


def gelu_parts(gated):
    tanh_arg = gelu_scale * (gated + 0.044715 * gated * gated * gated)
    tangent = jnp.tanh(tanh_arg)
    result_value = 0.5 * gated * (1.0 + tangent)
    derivative = 0.5 * (1.0 + tangent) + 0.5 * gated * (1.0 - tangent * tangent) * gelu_scale * (
        1.0 + 3.0 * 0.044715 * gated * gated
    )
    return (result_value, derivative)


def kernel(
    tok, cot, member, in_fast, out_fast, hidden_fast, mid_fast, wu, wd,
    lo, ug, dg, fin_in, fin_out, fin_mid, fin_hid,
    gx, xn, gc, dc, eye, tab_f, tab_own, hm_col, tabs, tabt, own_col, sel, selm, stats, col,
    pa, p_send, p_recv, h_send, h_recv, hid, upc,
    rf, rv, ruf, ru, rl, fb, bo_in,
    in_acc, in_recv, y_in, y_out, s_send, s_recv, mh_own, mh_all, ss, rs,
):
    h, c, y, x, l = [lax.axis_index(a) for a in AXES]
    here = dict(h=h, c=c, y=y, x=x, l=l)
    dp = 2 * h + c

    def at(**off):
        pos = dict(here)
        for axis, step in off.items():
            pos[axis] = lax.rem(pos[axis] + (step + SIZES[axis]), SIZES[axis])
        return tuple(pos[a] for a in AXES)

    partner = (y // 2, lax.rem(y, 2), dp, x, l)
    is_self = y == dp
    dp_parts = [at(c=1), at(h=1), at(h=1, c=1)]
    xl_parts = [(dx, dl) for dx in (0, 1, 2, 3) for dl in (0, 1) if dx or dl]
    y_parts = [1, 2, 3]

    counter = [0]
    sends = []

    def start(src, dst, dev):
        i = counter[0]
        counter[0] += 1
        copy = pltpu.make_async_remote_copy(
            src_ref=src, dst_ref=dst, send_sem=ss.at[i], recv_sem=rs.at[i],
            device_id=dev, device_id_type=MESH,
        )
        copy.start()
        sends.append(copy.wait_send)
        return copy

    def start_swap(src, dst):
        i = counter[0]
        counter[0] += 1
        copy = pltpu.make_async_remote_copy(
            src_ref=src, dst_ref=dst, send_sem=ss.at[i], recv_sem=rs.at[i],
            device_id=partner, device_id_type=MESH,
        )

        @pl.when(jnp.logical_not(is_self))
        def _():
            copy.start()

        @pl.when(is_self)
        def _():
            pltpu.make_async_copy(src, dst, rs.at[i]).start()

        def wait_send():
            @pl.when(jnp.logical_not(is_self))
            def _():
                copy.wait_send()

        sends.append(wait_send)
        return copy

    def drain(waits):
        for wait in waits:
            wait()
        waits.clear()

    bar = pltpu.get_barrier_semaphore()
    greet = dp_parts + [at(x=dx, l=dl) for dx, dl in xl_parts] + [at(y=dy) for dy in y_parts]
    for dev in greet:
        pl.semaphore_signal(bar, inc=1, device_id=dev, device_id_type=MESH)

    @pl.when(jnp.logical_not(is_self))
    def _():
        pl.semaphore_signal(bar, inc=1, device_id=partner, device_id_type=MESH)

    member_row = lax.broadcasted_iota(jnp.int32, (16, IMG), 0)
    for i in (0, 1):
        for t in (0, 1):
            sel[2 * dp + i, t] = jnp.where(member_row == member[i] + 8 * t, 1.0, 0.0).astype(BF16)
    tab_f[...] = jnp.zeros((16, FFB), F32)
    tab_f[0:4, 0:PIECE] = in_fast[...].astype(F32)
    tab_f[8:12, 0:PIECE] = out_fast[...].astype(F32)
    tab_own[...] = tab_f[:, 0:IMG].astype(BF16)

    pl.semaphore_wait(bar, jnp.where(is_self, len(greet), len(greet) + 1))

    own_piece = 2 * x + l
    own_rows = pl.ds(pl.multiple_of(PIECE * own_piece, PIECE), PIECE)

    lanes = [pl.ds(0, IMG), pl.ds(IMG, IMG)]
    swap_x = [start_swap(tok.at[:, lanes[j]], gx.at[2 * dp + j, own_rows]) for j in (0, 1)]
    swap_tab = start_swap(tab_own, tabs.at[own_piece])
    sel_mine = sel.at[pl.ds(2 * dp, 2)]
    sel_copies = [start(sel_mine, sel_mine, dev) for dev in dp_parts]
    swap_c = [start_swap(cot.at[:, lanes[j]], gc.at[2 * dp + j, own_rows]) for j in (0, 1)]

    def image(j, dy):
        return 2 * lax.rem(y + (dy + 4), 4) + j

    def chunk(ref, j, du, dv, q=None):
        dy, dx = (dv, du) if j == 0 else (du, dv)
        row = PAIR * lax.rem(x + (dx + 4), 4)
        size = PAIR
        if q is not None:
            row, size = row + PIECE * q, PIECE
        return ref.at[image(j, dy), pl.ds(pl.multiple_of(row, PIECE), size)]

    def u_dev(j, step):
        return at(x=step) if j == 0 else at(y=step)

    def v_dev(j, step):
        return at(y=step) if j == 0 else at(x=step)

    both = (0, 1)

    def gather(buf, swaps):
        r = [dict(), dict()]

        def u_send(j, du, q, step, name):
            piece = chunk(buf, j, du, 0, q)
            r[j][name] = start(piece, piece, u_dev(j, step))

        def v_send(j, du, dv, step, name):
            part = chunk(buf, j, du, dv)
            r[j][name] = start(part, part, v_dev(j, step))

        for j in both:
            swaps[j].wait_recv()
            piece = chunk(buf, j, 0, 0, l)
            r[j]["l"] = start(piece, piece, at(l=1))
            u_send(j, 0, l, 1, "-own")
            u_send(j, 0, l, -1, "+own")
        yield
        for j in both:
            r[j]["l"].wait_recv()
            u_send(j, 0, 1 - l, 1, "-oth")
            u_send(j, 0, 1 - l, -1, "+oth")
        for j in both:
            r[j]["-own"].wait_recv()
            u_send(j, -1, l, 1, "fwd-")
        for j in both:
            v_send(j, 0, 0, 1, "v-0")
            v_send(j, 0, 0, -1, "v+0")
        yield
        for j in both:
            r[j]["+own"].wait_recv()
            r[j]["+oth"].wait_recv()
            u_send(j, 1, 1 - l, -1, "fwd+")
            v_send(j, 1, 0, 1, "v-1")
            v_send(j, 1, 0, -1, "v+1")
            r[j]["-oth"].wait_recv()
            v_send(j, -1, 0, 1, "v-m")
            v_send(j, -1, 0, -1, "v+m")
        yield
        for j in both:
            r[j]["fwd-"].wait_recv()
            r[j]["fwd+"].wait_recv()
            v_send(j, 2, 0, 1, "v-2")
            v_send(j, 2, 0, -1, "v+2")
        yield
        for j in both:
            r[j]["v-0"].wait_recv()
            v_send(j, 0, -1, 1, "w-0")
            r[j]["v+1"].wait_recv()
            v_send(j, 1, 1, -1, "w+1")
        yield
        for j in both:
            r[j]["v-m"].wait_recv()
            v_send(j, -1, -1, 1, "w-m")
            r[j]["v+2"].wait_recv()
            v_send(j, 2, 1, -1, "w+2")
        yield
        for name in ("v+0", "v+m", "v-1", "v-2"):
            for j in both:
                r[j][name].wait_recv()
        r[1]["w-0"].wait_recv()
        yield
        for name in ("w-0", "w+1", "w-m", "w+2"):
            for j in both:
                if (j, name) != (1, "w-0"):
                    r[j][name].wait_recv()
        yield

    def run(gen, steps=1000):
        for _ in range(steps):
            if next(gen, "end") == "end":
                return

    first = [image(0, 0)]
    second = [image(1, 0), image(0, -1), image(0, 1)]
    third = [image(1, -1), image(1, 1), image(0, 2), image(1, 2)]
    order = first + second + third

    run_x = gather(gx, swap_x)
    run_c = gather(gc, swap_c)
    run(run_x, 1)

    swap_tab.wait_recv()
    tab_copies = [
        start(tabs.at[own_piece], tabs.at[own_piece], at(x=dx, l=dl)) for dx, dl in xl_parts
    ]
    run(run_x, 1)
    ident = lax.broadcasted_iota(jnp.int32, (FFB, FFB), 0) == lax.broadcasted_iota(
        jnp.int32, (FFB, FFB), 1
    )
    eye[...] = jnp.where(ident, 1.0, 0.0).astype(BF16)
    run(run_x, 1)
    own_col[...] = dot_t(eye[:PIECE, :IMG], tab_own[...]).astype(BF16)
    tab_f[0:4, :] = hidden_fast[...].astype(F32)
    tab_f[8:12, :] = mid_fast[...].astype(F32)
    hm_col[...] = dot_t(eye[...], tab_f[...].astype(BF16)).astype(BF16)
    col[...] = jnp.zeros((D_BLK, 128), F32)
    run(run_x, 1)
    for copy in sel_copies:
        copy.wait_recv()
    for copy in tab_copies:
        copy.wait_recv()
    for p in range(8):
        tabt[p * PIECE : (p + 1) * PIECE, :] = dot_t(eye[:PIECE, :IMG], tabs[p]).astype(BF16)
    lane = lax.broadcasted_iota(jnp.int32, (16, 128), 1)
    picks = jnp.zeros((16, 128), F32)
    for img in range(N_IMG):
        picks = jnp.where(lane == img, sel[img, 0][:, 0:128].astype(F32), picks)
    selm[...] = picks

    stat_copies = {}
    stat_row = lax.broadcasted_iota(jnp.int32, (8, IMG), 0)

    def image_stats(n):
        img = order[n]

        def total(p, acc):
            rows = pl.ds(pl.multiple_of(p * PIECE, PIECE), PIECE)
            v = gx[img, rows].astype(F32).reshape(PIECE // 8, 8, IMG)
            return acc + jnp.sum(v, axis=0)

        def spread(p, acc):
            rows = pl.ds(pl.multiple_of(p * PIECE, PIECE), PIECE)
            v = (gx[img, rows].astype(F32) - mean).reshape(PIECE // 8, 8, IMG)
            return acc + jnp.sum(v * v, axis=0)

        zero = jnp.zeros((8, IMG), F32)
        mean = jnp.sum(lax.fori_loop(0, 8, total, zero), axis=0, keepdims=True) / D_BLK
        dev2 = jnp.sum(lax.fori_loop(0, 8, spread, zero), axis=0, keepdims=True)
        stats[dp, img] = jnp.where(stat_row == 0, mean, jnp.where(stat_row == 1, dev2, 0.0))
        part = stats.at[dp, img]
        stat_copies[n] = [start(part, part, dev) for dev in dp_parts]

    def normalise(n):
        img = order[n]
        for copy in stat_copies[n]:
            copy.wait_recv()
        parts = [stats[k, img] for k in range(4)]
        mean = (parts[0][0:1] + parts[1][0:1] + parts[2][0:1] + parts[3][0:1]) * 0.25
        dev2 = parts[0][1:2] + parts[1][1:2] + parts[2][1:2] + parts[3][1:2]
        for k in range(4):
            gap = parts[k][0:1] - mean
            dev2 = dev2 + D_BLK * (gap * gap)
        rstd = lax.rsqrt(dev2 / (4 * D_BLK) + 1e-06)
        factor = dot(tabt[...], sel[img, 0])
        xn[img] = ((gx[img].astype(F32) - mean) * rstd * factor).astype(BF16)

    mine = pl.ds(pl.multiple_of(HALF * c, HALF), HALF)
    other = pl.ds(pl.multiple_of(HALF * (1 - c), HALF), HALF)
    core = at(c=1)
    far = at(h=1)
    near = [dict(), dict()]
    wide = [dict(), dict()]

    def partial_product(m, weight, operand, n):
        img = order[n]
        part = lax.dot_general(
            weight[...], operand[img], (((0,), (0,)), ((), ())), preferred_element_type=F32
        )
        low, high = part[0:HALF], part[HALF:FFB]
        p_send[m, img] = jnp.where(c == 0, high, low).astype(BF16)
        near[m][n] = start(p_send.at[m, img], p_recv.at[m, img], core)
        pa[m, img] = jnp.where(c == 0, low, high)

    def to_far(m, n):
        img = order[n]
        near[m][n].wait_recv()
        total = pa[m, img] + p_recv[m, img].astype(F32)
        pa[m, img] = total
        h_send[m, img] = total.astype(BF16)
        wide[m][n] = start(h_send.at[m, img], h_recv.at[m, img], far)

    hid_copies, upc_copies = {}, {}

    def finish_hidden(n):
        img = order[n]
        wide[0][n].wait_recv()
        pre_act = pa[0, img] + h_recv[0, img].astype(F32)
        pa[0, img] = pre_act
        hid_row = dot(hm_col[mine, :], sel[img, 0])
        mid_row = dot(hm_col[mine, :], sel[img, 1])
        activated, _ = gelu_parts(pre_act * hid_row)
        hid[img, mine] = (activated * mid_row).astype(BF16)
        hid_copies[n] = start(hid.at[img, mine], hid.at[img, mine], core)

    br = gx

    def branch_part(n):
        img = order[n]
        hid_copies[n].wait_recv()
        br[img] = dot(wd[...], hid[img]).astype(BF16)

    def forward(n):
        normalise(n)
        partial_product(0, wu, xn, n)

    run(run_x, 2)
    image_stats(0)
    run(run_c, 1)
    run(run_x, 1)
    for n in (1, 2, 3):
        image_stats(n)
    forward(0)
    run(run_c, 1)
    forward(1)
    to_far(0, 0)
    run(run_x, 1)
    x_sends = list(sends)
    sends.clear()
    for n in (4, 5, 6, 7):
        image_stats(n)
    forward(2)
    to_far(0, 1)
    forward(3)
    to_far(0, 2)
    run(run_c, 1)
    finish_hidden(0)
    for n in (4, 5, 6, 7):
        forward(n)
        to_far(0, n - 1)
        finish_hidden(n - 3)
    run(run_c, 1)
    to_far(0, 7)
    finish_hidden(5)
    drain(x_sends)
    run(run_c, 1)
    for n in (0, 1, 2):
        branch_part(n)
    finish_hidden(6)
    for n in (3, 4, 5):
        branch_part(n)
    finish_hidden(7)
    run(run_c, 1)
    for n in (6, 7):
        branch_part(n)

    up, down = (0, -1), (1, 2)
    slot = {0: 0, -1: 1, 1: 2, 2: 3}

    def add_into(dst, *terms):
        total = dst[...].astype(F32)
        for term in terms:
            total = total + term[...].astype(F32)
        dst[...] = total.astype(BF16)

    finals = []

    def scatter():
        r = [dict(), dict()]
        for j in both:
            for i in (0, 1):
                r[j]["f+", up[i]] = start(chunk(br, j, up[i], 2), rf.at[j, 0, i], v_dev(j, 1))
                r[j]["f-", down[i]] = start(chunk(br, j, down[i], 2), rf.at[j, 1, i], v_dev(j, -1))
        for j in both:
            for k in (2, 1):
                r[j]["d+", k] = start(chunk(br, j, k, 1), rv.at[j, 0, slot[k]], v_dev(j, 1))
            for k in (-1, 0):
                r[j]["d-", k] = start(chunk(br, j, k, -1), rv.at[j, 1, slot[k]], v_dev(j, -1))
        yield
        for i in (1, 0):
            for j in both:
                r[j]["f+", up[i]].wait_recv()
                part = chunk(br, j, up[i], 1)
                add_into(part, rf.at[j, 0, i])
                r[j]["d+", up[i]] = start(part, rv.at[j, 0, slot[up[i]]], v_dev(j, 1))
                r[j]["f-", down[i]].wait_recv()
                part = chunk(br, j, down[i], -1)
                add_into(part, rf.at[j, 1, i])
                r[j]["d-", down[i]] = start(part, rv.at[j, 1, slot[down[i]]], v_dev(j, -1))
            yield

        def total(j, k):
            r[j]["d+", k].wait_recv()
            r[j]["d-", k].wait_recv()
            part = chunk(br, j, k, 0)
            add_into(part, rv.at[j, 0, slot[k]], rv.at[j, 1, slot[k]])

        for j in both:
            total(j, 2)
            r[j]["uf+"] = start(chunk(br, j, 2, 0, 0), ruf.at[j, 0], u_dev(j, 1))
            r[j]["uf-"] = start(chunk(br, j, 2, 0, 1), ruf.at[j, 1], u_dev(j, -1))
        yield
        low, high = pl.ds(0, PIECE), pl.ds(PIECE, PIECE)
        for j in both:
            total(j, -1)
            r[j]["u-0"] = start(chunk(br, j, -1, 0, 0), ru.at[j, 1, low], u_dev(j, -1))
        for j in both:
            total(j, 1)
            r[j]["u+1"] = start(chunk(br, j, 1, 0, 1), ru.at[j, 0, high], u_dev(j, 1))
        yield
        for j in both:
            r[j]["uf+"].wait_recv()
            part = chunk(br, j, 1, 0, 0)
            add_into(part, ruf.at[j, 0])
            r[j]["u+0"] = start(part, ru.at[j, 0, low], u_dev(j, 1))
            r[j]["uf-"].wait_recv()
            part = chunk(br, j, -1, 0, 1)
            add_into(part, ruf.at[j, 1])
            r[j]["u-1"] = start(part, ru.at[j, 1, high], u_dev(j, -1))
        for j in both:
            total(j, 0)
        yield
        for j in both:
            for name in ("u+1", "u+0", "u-0", "u-1"):
                r[j][name].wait_recv()
            add_into(chunk(br, j, 0, 0), ru.at[j, 0], ru.at[j, 1])
            r[j]["l"] = start(chunk(br, j, 0, 0, 1 - l), rl.at[j], at(l=1))
        yield
        for j in both:
            r[j]["l"].wait_recv()
            piece = chunk(br, j, 0, 0, l)[...].astype(F32) + rl[j].astype(F32)
            fb[j] = piece.astype(BF16)
            finals.append(start_swap(fb.at[j], bo_in.at[j]))
        yield

    run_s = scatter()
    run(run_s, 1)

    def backward(n):
        img = order[n]
        factor = dot(tabt[...], sel[img, 1])
        dc[img] = (gc[img].astype(F32) * factor).astype(BF16)
        partial_product(1, wd, dc, n)

    mh_own[...] = jnp.zeros((32, IMG), F32)

    def finish_cot(n):
        img = order[n]
        wide[1][n].wait_recv()
        grad_act = pa[1, img] + h_recv[1, img].astype(F32)
        pre_act = pa[0, img]
        hid_row = dot(hm_col[mine, :], sel[img, 0])
        mid_row = dot(hm_col[mine, :], sel[img, 1])
        activated, derivative = gelu_parts(pre_act * hid_row)
        grad_gated = grad_act * mid_row * derivative
        upc[img, mine] = (grad_gated * hid_row).astype(BF16)
        upc_copies[n] = start(upc.at[img, mine], upc.at[img, mine], core)
        pick = sel[img, 0]
        mh_own[0:16, 0:HALF] += dot_t(pick, (activated * grad_act).astype(BF16))
        mh_own[16:32, 0:HALF] += dot_t(pick, (pre_act * grad_gated).astype(BF16))

    def down_rows(k):
        rows = pl.ds(k * PAIR, PAIR)
        acc = dot_t(dc[0, rows], hid[0])
        for img in range(1, 8):
            acc = acc + dot_t(dc[img, rows], hid[img])
        dg[rows, :] = acc.astype(BF16)

    def up_rows(k):
        rows = pl.ds(k * PAIR, PAIR)
        weight = wu[rows, :].astype(F32)
        acc = jnp.zeros((PAIR, FFB), F32)
        for img in range(8):
            part = dot_t(xn[img, rows], upc[img])
            acc = acc + part
            col[rows, img : img + 1] = jnp.sum(part * weight, axis=1, keepdims=True)
        ug[rows, :] = acc.astype(BF16)

    backward(0)
    run(run_c, 1)
    to_far(1, 0)
    for n in (1, 2, 3):
        backward(n)
        if n > 1:
            to_far(1, n - 1)
    run(run_c, 1)
    to_far(1, 3)
    for n in (4, 5, 6, 7):
        backward(n)
        if n > 4:
            to_far(1, n - 1)
        finish_cot(n - 4)
    to_far(1, 7)
    run(run_s, 1)
    down_rows(0)
    finish_cot(4)
    run(run_s, 1)
    down_rows(1)
    finish_cot(5)
    down_rows(2)
    finish_cot(6)
    down_rows(3)
    finish_cot(7)
    mh_all[dp] = mh_own[...]
    mh_copies = [start(mh_own, mh_all.at[dp], dev) for dev in dp_parts]
    for n in range(8):
        upc_copies[n].wait_recv()
    up_rows(0)
    run(run_s, 1)
    up_rows(1)
    up_rows(2)
    run(run_s, 1)
    up_rows(3)
    run(run_s, 1)

    in_acc[...] = jnp.zeros((8, 16, IMG), F32)
    for p in range(8):
        in_acc[p, :, 0:PIECE] = lax.dot_general(
            selm[...], col[p * PIECE : (p + 1) * PIECE, :], (((1,), (1,)), ((), ())),
            precision=lax.Precision.HIGHEST, preferred_element_type=F32,
        )
    in_copies = []
    for i, (dx, dl) in enumerate(xl_parts):
        p_to = 2 * lax.rem(x + dx, 4) + lax.rem(l + dl, 2)
        in_copies.append(start(in_acc.at[p_to], in_recv.at[i], at(x=dx, l=dl)))
    run(run_s, 1)
    for copy in in_copies:
        copy.wait_recv()
    total_in = in_acc[own_piece]
    for i in range(7):
        total_in = total_in + in_recv[i]
    y_in[y] = total_in
    y_in_copies = [start(y_in.at[y], y_in.at[y], at(y=dy)) for dy in y_parts]
    run(run_s)

    out_total = jnp.zeros((16, PIECE), F32)
    for j in both:
        prod = gc[2 * y + j, own_rows].astype(F32) * fb[j].astype(F32)
        out_total = out_total + dot_t(sel[2 * y + j, 0], prod.astype(BF16))
    y_out[y] = jnp.zeros((16, IMG), F32)
    y_out[y, :, 0:PIECE] = out_total
    y_out_copies = [start(y_out.at[y], y_out.at[y], at(y=dy)) for dy in y_parts]
    for copy in y_in_copies + y_out_copies:
        copy.wait_recv()
    s_send[0] = (y_in[0] + y_in[1]) + (y_in[2] + y_in[3])
    s_send[1] = (y_out[0] + y_out[1]) + (y_out[2] + y_out[3])
    last = start_swap(s_send, s_recv)
    for copy in mh_copies:
        copy.wait_recv()
    fin_mid[...] = jnp.concatenate([mh_all[0, 0:4, 0:HALF], mh_all[1, 0:4, 0:HALF]], axis=1)
    fin_hid[...] = jnp.concatenate([mh_all[0, 16:20, 0:HALF], mh_all[1, 16:20, 0:HALF]], axis=1)
    for j in both:
        finals[j].wait_recv()
        factor = dot(own_col[...], sel[2 * dp + j, 1])
        lo[:, lanes[j]] = (
            tok[:, lanes[j]].astype(F32) + bo_in[j].astype(F32) * factor
        ).astype(BF16)
    last.wait_recv()
    fin_in[...] = s_recv[0, 0:4, 0:PIECE] / in_fast[...].astype(F32)
    fin_out[...] = s_recv[1, 0:4, 0:PIECE]
    drain(sends)


def exchange(*arrays):
    vmem = pl.BlockSpec(memory_space=pltpu.VMEM)
    smem = pl.BlockSpec(memory_space=pltpu.SMEM)
    out_shape = [
        jax.ShapeDtypeStruct((PIECE, 2 * IMG), BF16),
        jax.ShapeDtypeStruct((D_BLK, FFB), BF16),
        jax.ShapeDtypeStruct((D_BLK, FFB), BF16),
        jax.ShapeDtypeStruct((4, PIECE), F32),
        jax.ShapeDtypeStruct((4, PIECE), F32),
        jax.ShapeDtypeStruct((4, FFB), F32),
        jax.ShapeDtypeStruct((4, FFB), F32),
    ]
    scratch = [
        ((N_IMG, D_BLK, IMG), BF16),
        ((N_IMG, D_BLK, IMG), BF16),
        ((N_IMG, D_BLK, IMG), BF16),
        ((N_IMG, D_BLK, IMG), BF16),
        ((FFB, FFB), BF16),
        ((16, FFB), F32),
        ((16, IMG), BF16),
        ((FFB, 16), BF16),
        ((8, 16, IMG), BF16),
        ((D_BLK, 16), BF16),
        ((PIECE, 16), BF16),
        ((N_IMG, 2, 16, IMG), BF16),
        ((16, 128), F32),
        ((4, N_IMG, 8, IMG), F32),
        ((D_BLK, 128), F32),
        ((2, N_IMG, HALF, IMG), F32),
        ((2, N_IMG, HALF, IMG), BF16),
        ((2, N_IMG, HALF, IMG), BF16),
        ((2, N_IMG, HALF, IMG), BF16),
        ((2, N_IMG, HALF, IMG), BF16),
        ((N_IMG, FFB, IMG), BF16),
        ((N_IMG, FFB, IMG), BF16),
        ((2, 2, 2, PAIR, IMG), BF16),
        ((2, 2, 4, PAIR, IMG), BF16),
        ((2, 2, PIECE, IMG), BF16),
        ((2, 2, PAIR, IMG), BF16),
        ((2, PIECE, IMG), BF16),
        ((2, PIECE, IMG), BF16),
        ((2, PIECE, IMG), BF16),
        ((8, 16, IMG), F32),
        ((7, 16, IMG), F32),
        ((4, 16, IMG), F32),
        ((4, 16, IMG), F32),
        ((2, 16, IMG), F32),
        ((2, 16, IMG), F32),
        ((32, IMG), F32),
        ((4, 32, IMG), F32),
    ]
    return pl.pallas_call(
        kernel,
        out_shape=out_shape,
        in_specs=[vmem, vmem, smem] + [vmem] * 6,
        out_specs=[vmem] * 7,
        scratch_shapes=[pltpu.VMEM(s, d) for s, d in scratch]
        + [pltpu.SemaphoreType.DMA((N_SEM,)), pltpu.SemaphoreType.DMA((N_SEM,))],
        compiler_params=pltpu.CompilerParams(
            collective_id=0, has_side_effects=True, vmem_limit_bytes=62 * 1024 * 1024
        ),
        cost_estimate=pl.CostEstimate(
            flops=14_500_000_000, bytes_accessed=12_000_000, transcendentals=1_600_000
        ),
    )(*arrays)


def body(
    tokens, member, up_weight, down_weight, in_fast, hidden_fast, mid_fast, out_fast, cotangent
):
    lo, ug, dg, in_grad, out_grad, mid_grad, hidden_grad = exchange(
        tokens.T, cotangent.T, member, in_fast, out_fast, hidden_fast, mid_fast,
        up_weight, down_weight,
    )
    return (lo.T, ug.astype(F32), dg.astype(F32), in_grad, hidden_grad, mid_grad, out_grad)


def solution(mesh):
    grid = Mesh(mesh.devices.reshape([SIZES[a] for a in AXES]), AXES)
    dp, mp = ("h", "c"), ("y", "x", "l")
    in_specs = (
        P(dp, mp),
        P(dp),
        P(dp, mp),
        P(dp, mp),
        P(None, mp),
        P(None, mp),
        P(None, mp),
        P(None, mp),
        P(dp, mp),
    )
    out_specs = (
        P(dp, mp),
        P(dp, mp),
        P(dp, mp),
        P(None, mp),
        P(None, mp),
        P(None, mp),
        P(None, mp),
    )
    return jax.shard_map(body, mesh=grid, in_specs=in_specs, out_specs=out_specs, check_vma=False)
```

```python
import math

import jax
import jax.numpy as jnp
from jax import lax
from jax.experimental import pallas as pl
from jax.experimental.pallas import tpu as pltpu
from jax.sharding import Mesh
from jax.sharding import PartitionSpec as P

AXES = ("h", "c", "y", "x", "l")
SIZES = dict(h=2, c=2, y=4, x=4, l=2)
MESH = pl.DeviceIdType.MESH
F32 = jnp.float32
BF16 = jnp.bfloat16
gelu_scale = math.sqrt(2.0 / math.pi)

D_BLK = 1536
PIECE = 192
PAIR = 384
IMG = 256
N_IMG = 8
FFB = 384
HALF = 192
N_SEM = 240


def dot(a, b):
    return jnp.dot(a, b, preferred_element_type=F32)


def dot_t(a, b):
    return lax.dot_general(a, b, (((1,), (1,)), ((), ())), preferred_element_type=F32)


def gelu_parts(gated):
    tanh_arg = gelu_scale * (gated + 0.044715 * gated * gated * gated)
    tangent = jnp.tanh(tanh_arg)
    result_value = 0.5 * gated * (1.0 + tangent)
    derivative = 0.5 * (1.0 + tangent) + 0.5 * gated * (1.0 - tangent * tangent) * gelu_scale * (
        1.0 + 3.0 * 0.044715 * gated * gated
    )
    return (result_value, derivative)


def kernel(
    tok, cot, member, in_fast, out_fast, hidden_fast, mid_fast, wu, wd,
    lo, ug, dg, fin_in, fin_out, fin_mid, fin_hid,
    gx, xn, gc, dc, eye, tab_f, tab_own, hm_col, tabs, tabt, own_col, sel, selm, st_own, st_xl, st_y, stats, col,
    pa, p_send, p_recv, h_send, h_recv, hid, upc,
    rf, rv, ruf, ru, rl, fb, bo_in,
    in_acc, in_recv, y_in, y_out, s_send, s_recv, mh_own, mh_all, ss, rs,
):
    h, c, y, x, l = [lax.axis_index(a) for a in AXES]
    here = dict(h=h, c=c, y=y, x=x, l=l)
    dp = 2 * h + c

    def at(**off):
        pos = dict(here)
        for axis, step in off.items():
            pos[axis] = lax.rem(pos[axis] + (step + SIZES[axis]), SIZES[axis])
        return tuple(pos[a] for a in AXES)

    partner = (y // 2, lax.rem(y, 2), dp, x, l)
    is_self = y == dp
    dp_parts = [at(c=1), at(h=1), at(h=1, c=1)]
    xl_parts = [(dx, dl) for dx in (0, 1, 2, 3) for dl in (0, 1) if dx or dl]
    y_parts = [1, 2, 3]

    counter = [0]
    sends = []

    def start(src, dst, dev):
        i = counter[0]
        counter[0] += 1
        copy = pltpu.make_async_remote_copy(
            src_ref=src, dst_ref=dst, send_sem=ss.at[i], recv_sem=rs.at[i],
            device_id=dev, device_id_type=MESH,
        )
        copy.start()
        sends.append(copy.wait_send)
        return copy

    def start_swap(src, dst):
        i = counter[0]
        counter[0] += 1
        copy = pltpu.make_async_remote_copy(
            src_ref=src, dst_ref=dst, send_sem=ss.at[i], recv_sem=rs.at[i],
            device_id=partner, device_id_type=MESH,
        )

        @pl.when(jnp.logical_not(is_self))
        def _():
            copy.start()

        @pl.when(is_self)
        def _():
            pltpu.make_async_copy(src, dst, rs.at[i]).start()

        def wait_send():
            @pl.when(jnp.logical_not(is_self))
            def _():
                copy.wait_send()

        sends.append(wait_send)
        return copy

    def drain(waits):
        for wait in waits:
            wait()
        waits.clear()

    bar = pltpu.get_barrier_semaphore()
    greet = dp_parts + [at(x=dx, l=dl) for dx, dl in xl_parts] + [at(y=dy) for dy in y_parts]
    for dev in greet:
        pl.semaphore_signal(bar, inc=1, device_id=dev, device_id_type=MESH)

    @pl.when(jnp.logical_not(is_self))
    def _():
        pl.semaphore_signal(bar, inc=1, device_id=partner, device_id_type=MESH)

    member_row = lax.broadcasted_iota(jnp.int32, (16, IMG), 0)
    for i in (0, 1):
        for t in (0, 1):
            sel[2 * dp + i, t] = jnp.where(member_row == member[i] + 8 * t, 1.0, 0.0).astype(BF16)
    tab_f[...] = jnp.zeros((16, FFB), F32)
    tab_f[0:4, 0:PIECE] = in_fast[...].astype(F32)
    tab_f[8:12, 0:PIECE] = out_fast[...].astype(F32)
    tab_own[...] = tab_f[:, 0:IMG].astype(BF16)

    pl.semaphore_wait(bar, jnp.where(is_self, len(greet), len(greet) + 1))

    own_piece = 2 * x + l
    own_rows = pl.ds(pl.multiple_of(PIECE * own_piece, PIECE), PIECE)

    lanes = [pl.ds(0, IMG), pl.ds(IMG, IMG)]
    swap_x = [start_swap(tok.at[:, lanes[j]], gx.at[2 * dp + j, own_rows]) for j in (0, 1)]
    swap_tab = start_swap(tab_own, tabs.at[own_piece])
    sel_mine = sel.at[pl.ds(2 * dp, 2)]
    sel_copies = [start(sel_mine, sel_mine, dev) for dev in dp_parts]

    def image(j, dy):
        return 2 * lax.rem(y + (dy + 4), 4) + j

    def chunk(ref, j, du, dv, q=None):
        dy, dx = (dv, du) if j == 0 else (du, dv)
        row = PAIR * lax.rem(x + (dx + 4), 4)
        size = PAIR
        if q is not None:
            row, size = row + PIECE * q, PIECE
        return ref.at[image(j, dy), pl.ds(pl.multiple_of(row, PIECE), size)]

    def u_dev(j, step):
        return at(x=step) if j == 0 else at(y=step)

    def v_dev(j, step):
        return at(y=step) if j == 0 else at(x=step)

    both = (0, 1)

    def gather(buf, swaps, mate):
        r = [dict(), dict()]

        def u_send(j, du, q, step, name):
            piece = chunk(buf, j, du, 0, q)
            r[j][name] = start(piece, piece, u_dev(j, step))

        def v_send(j, du, dv, step, name):
            part = chunk(buf, j, du, dv)
            r[j][name] = start(part, part, v_dev(j, step))

        def own_send(j, dv, step, name):
            piece = chunk(buf, j, 0, dv, l)
            r[j][name] = start(piece, piece, v_dev(j, step))

        def mate_send(j, dv, name):
            piece = chunk(buf, j, 0, dv, l)
            r[j][name] = start(piece, piece, at(l=1))

        for j in both:
            swaps[j].wait_recv()
            mate_send(j, 0, "l")
            u_send(j, 0, l, 1, "-own")
            u_send(j, 0, l, -1, "+own")
            if mate:
                own_send(j, 0, 1, "v-0")
                own_send(j, 0, -1, "v+0")
        yield
        for j in both:
            r[j]["l"].wait_recv()
            u_send(j, 0, 1 - l, 1, "-oth")
            u_send(j, 0, 1 - l, -1, "+oth")
        for j in both:
            r[j]["-own"].wait_recv()
            u_send(j, -1, l, 1, "fwd-")
        for j in both:
            if mate:
                r[j]["v-0"].wait_recv()
                own_send(j, -1, 1, "w-0")
                mate_send(j, -1, "m-0")
                r[j]["v+0"].wait_recv()
                mate_send(j, 1, "m+0")
            else:
                v_send(j, 0, 0, 1, "v-0")
                v_send(j, 0, 0, -1, "v+0")
        yield
        for j in both:
            r[j]["+own"].wait_recv()
            r[j]["+oth"].wait_recv()
            u_send(j, 1, 1 - l, -1, "fwd+")
            v_send(j, 1, 0, 1, "v-1")
            v_send(j, 1, 0, -1, "v+1")
            r[j]["-oth"].wait_recv()
            v_send(j, -1, 0, 1, "v-m")
            v_send(j, -1, 0, -1, "v+m")
        yield
        for j in both:
            r[j]["fwd-"].wait_recv()
            r[j]["fwd+"].wait_recv()
            v_send(j, 2, 0, 1, "v-2")
            v_send(j, 2, 0, -1, "v+2")
        for j in both:
            if mate:
                r[j]["w-0"].wait_recv()
                mate_send(j, 2, "m2")
        yield
        for j in both:
            if not mate:
                r[j]["v-0"].wait_recv()
                v_send(j, 0, -1, 1, "w-0")
            r[j]["v+1"].wait_recv()
            v_send(j, 1, 1, -1, "w+1")
            r[j]["v-m"].wait_recv()
            v_send(j, -1, -1, 1, "w-m")
        yield
        for j in both:
            r[j]["v+2"].wait_recv()
            v_send(j, 2, 1, -1, "w+2")
        for j in both:
            if mate:
                r[j]["m-0"].wait_recv()
                r[j]["m+0"].wait_recv()
            else:
                r[j]["v+0"].wait_recv()
        last_own = "m2" if mate else "w-0"
        r[1][last_own].wait_recv()
        yield
        for name in ("v+m", "v-1", "v-2"):
            for j in both:
                r[j][name].wait_recv()
        r[0][last_own].wait_recv()
        yield
        for name in ("w+1", "w-m", "w+2"):
            for j in both:
                r[j][name].wait_recv()
        yield

    def run(gen, steps=1000):
        for _ in range(steps):
            if next(gen, "end") == "end":
                return

    first = [image(0, 0)]
    second = [image(1, 0), image(0, -1), image(0, 1)]
    third = [image(1, -1), image(1, 1), image(0, 2), image(1, 2)]
    order = first + second + third

    run_x = gather(gx, swap_x, True)

    stat_row = lax.broadcasted_iota(jnp.int32, (8, IMG), 0)

    def two_rows(first_row, second_row):
        return jnp.where(stat_row == 0, first_row, jnp.where(stat_row == 1, second_row, 0.0))

    def combine(parts, count):
        mean = sum(p[0:1] for p in parts) * (1.0 / len(parts))
        dev2 = sum(p[1:2] for p in parts)
        for p in parts:
            gap = p[0:1] - mean
            dev2 = dev2 + count * (gap * gap)
        return mean, dev2

    for j in both:
        values = tok[:, lanes[j]].astype(F32)
        mean = jnp.sum(values, axis=0, keepdims=True) * (1.0 / PIECE)
        gap = values - mean
        st_own[j] = two_rows(mean, jnp.sum(gap * gap, axis=0, keepdims=True))
    st_copies = [
        start(st_own, st_xl.at[i], at(x=dx, l=dl)) for i, (dx, dl) in enumerate(xl_parts)
    ]
    run(run_x, 1)

    swap_tab.wait_recv()
    tab_copies = [
        start(tabs.at[own_piece], tabs.at[own_piece], at(x=dx, l=dl)) for dx, dl in xl_parts
    ]
    for copy in st_copies:
        copy.wait_recv()
    for j in both:
        st_y[y, j] = two_rows(
            *combine([st_own[j]] + [st_xl[i, j] for i in range(7)], float(PIECE))
        )
    st_copies = [start(st_y.at[y], st_y.at[y], at(y=dy)) for dy in y_parts]
    run(run_x, 1)
    swap_c = [start_swap(cot.at[:, lanes[j]], gc.at[2 * dp + j, own_rows]) for j in (0, 1)]
    run_c = gather(gc, swap_c, False)
    ident = lax.broadcasted_iota(jnp.int32, (FFB, FFB), 0) == lax.broadcasted_iota(
        jnp.int32, (FFB, FFB), 1
    )
    eye[...] = jnp.where(ident, 1.0, 0.0).astype(BF16)
    run(run_x, 1)
    for copy in st_copies:
        copy.wait_recv()
    for j in both:
        mean, dev2 = combine([st_y[k, j] for k in range(4)], float(D_BLK))
        stats[2 * dp + j] = two_rows(mean, lax.rsqrt(dev2 / (4 * D_BLK) + 1e-06))
    stat_mine = stats.at[pl.ds(2 * dp, 2)]
    stat_copies = [start(stat_mine, stat_mine, dev) for dev in dp_parts]
    own_col[...] = dot_t(eye[:PIECE, :IMG], tab_own[...]).astype(BF16)
    tab_f[0:4, :] = hidden_fast[...].astype(F32)
    tab_f[8:12, :] = mid_fast[...].astype(F32)
    hm_col[...] = dot_t(eye[...], tab_f[...].astype(BF16)).astype(BF16)
    col[...] = jnp.zeros((D_BLK, 128), F32)
    run(run_x, 1)
    for copy in sel_copies + stat_copies:
        copy.wait_recv()
    for copy in tab_copies:
        copy.wait_recv()
    for p in range(8):
        tabt[p * PIECE : (p + 1) * PIECE, :] = dot_t(eye[:PIECE, :IMG], tabs[p]).astype(BF16)
    lane = lax.broadcasted_iota(jnp.int32, (16, 128), 1)
    picks = jnp.zeros((16, 128), F32)
    for img in range(N_IMG):
        picks = jnp.where(lane == img, sel[img, 0][:, 0:128].astype(F32), picks)
    selm[...] = picks

    def normalise(n):
        img = order[n]
        mean, rstd = stats[img, 0:1], stats[img, 1:2]
        factor = dot(tabt[...], sel[img, 0])
        xn[img] = ((gx[img].astype(F32) - mean) * rstd * factor).astype(BF16)

    mine = pl.ds(pl.multiple_of(HALF * c, HALF), HALF)
    other = pl.ds(pl.multiple_of(HALF * (1 - c), HALF), HALF)
    core = at(c=1)
    far = at(h=1)
    near = [dict(), dict()]
    wide = [dict(), dict()]

    def partial_product(m, weight, operand, n):
        img = order[n]
        part = lax.dot_general(
            weight[...], operand[img], (((0,), (0,)), ((), ())), preferred_element_type=F32
        )
        low, high = part[0:HALF], part[HALF:FFB]
        p_send[m, img] = jnp.where(c == 0, high, low).astype(BF16)
        near[m][n] = start(p_send.at[m, img], p_recv.at[m, img], core)
        pa[m, img] = jnp.where(c == 0, low, high)

    def to_far(m, n):
        img = order[n]
        near[m][n].wait_recv()
        total = pa[m, img] + p_recv[m, img].astype(F32)
        pa[m, img] = total
        h_send[m, img] = total.astype(BF16)
        wide[m][n] = start(h_send.at[m, img], h_recv.at[m, img], far)

    hid_copies, upc_copies = {}, {}

    def finish_hidden(n):
        img = order[n]
        wide[0][n].wait_recv()
        pre_act = pa[0, img] + h_recv[0, img].astype(F32)
        pa[0, img] = pre_act
        hid_row = dot(hm_col[mine, :], sel[img, 0])
        mid_row = dot(hm_col[mine, :], sel[img, 1])
        activated, _ = gelu_parts(pre_act * hid_row)
        hid[img, mine] = (activated * mid_row).astype(BF16)
        hid_copies[n] = start(hid.at[img, mine], hid.at[img, mine], core)

    br = gx

    def branch_part(n):
        img = order[n]
        hid_copies[n].wait_recv()
        br[img] = dot(wd[...], hid[img]).astype(BF16)

    def forward(n):
        normalise(n)
        partial_product(0, wu, xn, n)

    def backward(n):
        img = order[n]
        factor = dot(tabt[...], sel[img, 1])
        dc[img] = (gc[img].astype(F32) * factor).astype(BF16)
        partial_product(1, wd, dc, n)

    def each(step, *numbers):
        for n in numbers:
            step(n)

    forward(0)
    run(run_x, 1)
    to_far(0, 0)
    run(run_x, 1)
    forward(1)
    run(run_c, 1)
    to_far(0, 1)
    run(run_x, 1)
    forward(2)
    forward(3)
    to_far(0, 2)
    to_far(0, 3)
    run(run_x, 1)
    x_sends = list(sends)
    sends.clear()
    run(run_c, 1)
    forward(4)
    forward(5)
    to_far(0, 4)
    forward(6)
    to_far(0, 5)
    forward(7)
    to_far(0, 6)
    to_far(0, 7)
    run(run_c, 1)
    each(finish_hidden, 0, 1, 2, 3)
    run(run_c, 1)
    drain(x_sends)
    each(branch_part, 0, 1, 2, 3)
    finish_hidden(4)
    run(run_c, 1)
    finish_hidden(5)
    branch_part(4)
    finish_hidden(6)
    branch_part(5)
    run(run_c, 1)
    finish_hidden(7)
    branch_part(6)
    branch_part(7)

    up, down = (0, -1), (1, 2)
    slot = {0: 0, -1: 1, 1: 2, 2: 3}

    def add_into(dst, *terms):
        total = dst[...].astype(F32)
        for term in terms:
            total = total + term[...].astype(F32)
        dst[...] = total.astype(BF16)

    finals = []

    def scatter():
        r = [dict(), dict()]
        for j in both:
            for i in (0, 1):
                r[j]["f+", up[i]] = start(chunk(br, j, up[i], 2), rf.at[j, 0, i], v_dev(j, 1))
                r[j]["f-", down[i]] = start(chunk(br, j, down[i], 2), rf.at[j, 1, i], v_dev(j, -1))
        for j in both:
            for k in (2, 1):
                r[j]["d+", k] = start(chunk(br, j, k, 1), rv.at[j, 0, slot[k]], v_dev(j, 1))
            for k in (-1, 0):
                r[j]["d-", k] = start(chunk(br, j, k, -1), rv.at[j, 1, slot[k]], v_dev(j, -1))
        yield
        for i in (1, 0):
            for j in both:
                r[j]["f+", up[i]].wait_recv()
                part = chunk(br, j, up[i], 1)
                add_into(part, rf.at[j, 0, i])
                r[j]["d+", up[i]] = start(part, rv.at[j, 0, slot[up[i]]], v_dev(j, 1))
                r[j]["f-", down[i]].wait_recv()
                part = chunk(br, j, down[i], -1)
                add_into(part, rf.at[j, 1, i])
                r[j]["d-", down[i]] = start(part, rv.at[j, 1, slot[down[i]]], v_dev(j, -1))
            yield

        def total(j, k):
            r[j]["d+", k].wait_recv()
            r[j]["d-", k].wait_recv()
            part = chunk(br, j, k, 0)
            add_into(part, rv.at[j, 0, slot[k]], rv.at[j, 1, slot[k]])

        for j in both:
            total(j, 2)
            r[j]["uf+"] = start(chunk(br, j, 2, 0, 0), ruf.at[j, 0], u_dev(j, 1))
            r[j]["uf-"] = start(chunk(br, j, 2, 0, 1), ruf.at[j, 1], u_dev(j, -1))
        yield
        low, high = pl.ds(0, PIECE), pl.ds(PIECE, PIECE)
        for j in both:
            total(j, -1)
            r[j]["u-0"] = start(chunk(br, j, -1, 0, 0), ru.at[j, 1, low], u_dev(j, -1))
        for j in both:
            total(j, 1)
            r[j]["u+1"] = start(chunk(br, j, 1, 0, 1), ru.at[j, 0, high], u_dev(j, 1))
        yield
        for j in both:
            r[j]["uf+"].wait_recv()
            part = chunk(br, j, 1, 0, 0)
            add_into(part, ruf.at[j, 0])
            r[j]["u+0"] = start(part, ru.at[j, 0, low], u_dev(j, 1))
            r[j]["uf-"].wait_recv()
            part = chunk(br, j, -1, 0, 1)
            add_into(part, ruf.at[j, 1])
            r[j]["u-1"] = start(part, ru.at[j, 1, high], u_dev(j, -1))
        for j in both:
            total(j, 0)
        yield
        for j in both:
            for name in ("u+1", "u+0", "u-0", "u-1"):
                r[j][name].wait_recv()
            add_into(chunk(br, j, 0, 0), ru.at[j, 0], ru.at[j, 1])
            r[j]["l"] = start(chunk(br, j, 0, 0, 1 - l), rl.at[j], at(l=1))
        yield
        for j in both:
            r[j]["l"].wait_recv()
            piece = chunk(br, j, 0, 0, l)[...].astype(F32) + rl[j].astype(F32)
            fb[j] = piece.astype(BF16)
            finals.append(start_swap(fb.at[j], bo_in.at[j]))
        yield

    run_s = scatter()
    run(run_s, 1)

    mh_own[...] = jnp.zeros((32, IMG), F32)

    def finish_cot(n):
        img = order[n]
        wide[1][n].wait_recv()
        grad_act = pa[1, img] + h_recv[1, img].astype(F32)
        pre_act = pa[0, img]
        hid_row = dot(hm_col[mine, :], sel[img, 0])
        mid_row = dot(hm_col[mine, :], sel[img, 1])
        activated, derivative = gelu_parts(pre_act * hid_row)
        grad_gated = grad_act * mid_row * derivative
        upc[img, mine] = (grad_gated * hid_row).astype(BF16)
        upc_copies[n] = start(upc.at[img, mine], upc.at[img, mine], core)
        pick = sel[img, 0]
        mh_own[0:16, 0:HALF] += dot_t(pick, (activated * grad_act).astype(BF16))
        mh_own[16:32, 0:HALF] += dot_t(pick, (pre_act * grad_gated).astype(BF16))

    def down_rows(k):
        rows = pl.ds(k * PAIR, PAIR)
        acc = dot_t(dc[0, rows], hid[0])
        for img in range(1, 8):
            acc = acc + dot_t(dc[img, rows], hid[img])
        dg[rows, :] = acc.astype(BF16)

    def up_rows(k):
        rows = pl.ds(k * PAIR, PAIR)
        weight = wu[rows, :].astype(F32)
        acc = jnp.zeros((PAIR, FFB), F32)
        for img in range(8):
            part = dot_t(xn[img, rows], upc[img])
            acc = acc + part
            col[rows, img : img + 1] = jnp.sum(part * weight, axis=1, keepdims=True)
        ug[rows, :] = acc.astype(BF16)

    backward(0)
    backward(1)
    to_far(1, 0)
    run(run_c, 1)
    backward(2)
    to_far(1, 1)
    backward(3)
    to_far(1, 2)
    run(run_c, 1)
    for n in (4, 5, 6, 7):
        backward(n)
        to_far(1, n - 1)
    to_far(1, 7)
    run(run_s, 1)
    each(finish_cot, 0, 1)
    run(run_s, 1)
    each(finish_cot, 2, 3)
    down_rows(0)
    finish_cot(4)
    down_rows(1)
    run(run_s, 1)
    each(finish_cot, 5, 6, 7)
    mh_all[dp] = mh_own[...]
    mh_copies = [start(mh_own, mh_all.at[dp], dev) for dev in dp_parts]
    down_rows(2)
    run(run_s, 1)
    down_rows(3)
    for n in range(8):
        upc_copies[n].wait_recv()
    up_rows(0)
    run(run_s, 1)
    each(up_rows, 1, 2, 3)

    in_acc[...] = jnp.zeros((8, 16, IMG), F32)
    for p in range(8):
        in_acc[p, :, 0:PIECE] = lax.dot_general(
            selm[...], col[p * PIECE : (p + 1) * PIECE, :], (((1,), (1,)), ((), ())),
            precision=lax.Precision.HIGHEST, preferred_element_type=F32,
        )
    in_copies = []
    for i, (dx, dl) in enumerate(xl_parts):
        p_to = 2 * lax.rem(x + dx, 4) + lax.rem(l + dl, 2)
        in_copies.append(start(in_acc.at[p_to], in_recv.at[i], at(x=dx, l=dl)))
    run(run_s, 1)
    for copy in in_copies:
        copy.wait_recv()
    total_in = in_acc[own_piece]
    for i in range(7):
        total_in = total_in + in_recv[i]
    y_in[y] = total_in
    y_in_copies = [start(y_in.at[y], y_in.at[y], at(y=dy)) for dy in y_parts]
    run(run_s)

    out_total = jnp.zeros((16, PIECE), F32)
    for j in both:
        prod = gc[2 * y + j, own_rows].astype(F32) * fb[j].astype(F32)
        out_total = out_total + dot_t(sel[2 * y + j, 0], prod.astype(BF16))
    y_out[y] = jnp.zeros((16, IMG), F32)
    y_out[y, :, 0:PIECE] = out_total
    y_out_copies = [start(y_out.at[y], y_out.at[y], at(y=dy)) for dy in y_parts]
    for copy in y_in_copies + y_out_copies:
        copy.wait_recv()
    s_send[0] = (y_in[0] + y_in[1]) + (y_in[2] + y_in[3])
    s_send[1] = (y_out[0] + y_out[1]) + (y_out[2] + y_out[3])
    last = start_swap(s_send, s_recv)
    for copy in mh_copies:
        copy.wait_recv()
    fin_mid[...] = jnp.concatenate([mh_all[0, 0:4, 0:HALF], mh_all[1, 0:4, 0:HALF]], axis=1)
    fin_hid[...] = jnp.concatenate([mh_all[0, 16:20, 0:HALF], mh_all[1, 16:20, 0:HALF]], axis=1)
    for j in both:
        finals[j].wait_recv()
        factor = dot(own_col[...], sel[2 * dp + j, 1])
        lo[:, lanes[j]] = (
            tok[:, lanes[j]].astype(F32) + bo_in[j].astype(F32) * factor
        ).astype(BF16)
    last.wait_recv()
    fin_in[...] = s_recv[0, 0:4, 0:PIECE] / in_fast[...].astype(F32)
    fin_out[...] = s_recv[1, 0:4, 0:PIECE]
    drain(sends)


def widen(ug, dg, lo, *small):
    def copy(*refs):
        n = len(refs) // 2
        for src, dst in zip(refs[:n], refs[n:]):
            dst[...] = src[...].astype(dst.dtype)

    def spec(a, split):
        if split:
            return pl.BlockSpec((a.shape[0] // 4, a.shape[1]), lambda i: (i, 0))
        return pl.BlockSpec(a.shape, lambda i: (0, 0))

    arrays = (ug, dg, lo) + small
    specs = [spec(a, n < 2) for n, a in enumerate(arrays)]
    return pl.pallas_call(
        copy,
        grid=(4,),
        in_specs=specs,
        out_specs=specs,
        out_shape=[
            jax.ShapeDtypeStruct(a.shape, F32 if n < 2 else a.dtype)
            for n, a in enumerate(arrays)
        ],
    )(*arrays)


def exchange(*arrays):
    vmem = pl.BlockSpec(memory_space=pltpu.VMEM)
    smem = pl.BlockSpec(memory_space=pltpu.SMEM)
    out_shape = [
        jax.ShapeDtypeStruct((PIECE, 2 * IMG), BF16),
        jax.ShapeDtypeStruct((D_BLK, FFB), BF16),
        jax.ShapeDtypeStruct((D_BLK, FFB), BF16),
        jax.ShapeDtypeStruct((4, PIECE), F32),
        jax.ShapeDtypeStruct((4, PIECE), F32),
        jax.ShapeDtypeStruct((4, FFB), F32),
        jax.ShapeDtypeStruct((4, FFB), F32),
    ]
    scratch = [
        ((N_IMG, D_BLK, IMG), BF16),
        ((N_IMG, D_BLK, IMG), BF16),
        ((N_IMG, D_BLK, IMG), BF16),
        ((N_IMG, D_BLK, IMG), BF16),
        ((FFB, FFB), BF16),
        ((16, FFB), F32),
        ((16, IMG), BF16),
        ((FFB, 16), BF16),
        ((8, 16, IMG), BF16),
        ((D_BLK, 16), BF16),
        ((PIECE, 16), BF16),
        ((N_IMG, 2, 16, IMG), BF16),
        ((16, 128), F32),
        ((2, 8, IMG), F32),
        ((7, 2, 8, IMG), F32),
        ((4, 2, 8, IMG), F32),
        ((N_IMG, 8, IMG), F32),
        ((D_BLK, 128), F32),
        ((2, N_IMG, HALF, IMG), F32),
        ((2, N_IMG, HALF, IMG), BF16),
        ((2, N_IMG, HALF, IMG), BF16),
        ((2, N_IMG, HALF, IMG), BF16),
        ((2, N_IMG, HALF, IMG), BF16),
        ((N_IMG, FFB, IMG), BF16),
        ((N_IMG, FFB, IMG), BF16),
        ((2, 2, 2, PAIR, IMG), BF16),
        ((2, 2, 4, PAIR, IMG), BF16),
        ((2, 2, PIECE, IMG), BF16),
        ((2, 2, PAIR, IMG), BF16),
        ((2, PIECE, IMG), BF16),
        ((2, PIECE, IMG), BF16),
        ((2, PIECE, IMG), BF16),
        ((8, 16, IMG), F32),
        ((7, 16, IMG), F32),
        ((4, 16, IMG), F32),
        ((4, 16, IMG), F32),
        ((2, 16, IMG), F32),
        ((2, 16, IMG), F32),
        ((32, IMG), F32),
        ((4, 32, IMG), F32),
    ]
    return pl.pallas_call(
        kernel,
        out_shape=out_shape,
        in_specs=[vmem, vmem, smem] + [vmem] * 6,
        out_specs=[vmem] * 7,
        scratch_shapes=[pltpu.VMEM(s, d) for s, d in scratch]
        + [pltpu.SemaphoreType.DMA((N_SEM,)), pltpu.SemaphoreType.DMA((N_SEM,))],
        compiler_params=pltpu.CompilerParams(
            collective_id=0, has_side_effects=True, vmem_limit_bytes=62 * 1024 * 1024
        ),
        cost_estimate=pl.CostEstimate(
            flops=14_500_000_000, bytes_accessed=12_000_000, transcendentals=1_600_000
        ),
    )(*arrays)


def body(
    tokens, member, up_weight, down_weight, in_fast, hidden_fast, mid_fast, out_fast, cotangent
):
    lo, ug, dg, in_grad, out_grad, mid_grad, hidden_grad = exchange(
        tokens.T, cotangent.T, member, in_fast, out_fast, hidden_fast, mid_fast,
        up_weight, down_weight,
    )
    ug, dg, lo, in_grad, out_grad, mid_grad, hidden_grad = widen(
        ug, dg, lo, in_grad, out_grad, mid_grad, hidden_grad
    )
    return (lo.T, ug, dg, in_grad, hidden_grad, mid_grad, out_grad)


def solution(mesh):
    grid = Mesh(mesh.devices.reshape([SIZES[a] for a in AXES]), AXES)
    dp, mp = ("h", "c"), ("y", "x", "l")
    in_specs = (
        P(dp, mp),
        P(dp),
        P(dp, mp),
        P(dp, mp),
        P(None, mp),
        P(None, mp),
        P(None, mp),
        P(None, mp),
        P(dp, mp),
    )
    out_specs = (
        P(dp, mp),
        P(dp, mp),
        P(dp, mp),
        P(None, mp),
        P(None, mp),
        P(None, mp),
        P(None, mp),
    )
    return jax.shard_map(body, mesh=grid, in_specs=in_specs, out_specs=out_specs, check_vma=False)
```

```python
import math

import jax
import jax.numpy as jnp
from jax import lax
from jax.experimental import pallas as pl
from jax.experimental.pallas import tpu as pltpu
from jax.sharding import Mesh
from jax.sharding import PartitionSpec as P

AXES = ("h", "c", "y", "x", "l")
SIZES = dict(h=2, c=2, y=4, x=4, l=2)
MESH = pl.DeviceIdType.MESH
F32 = jnp.float32
BF16 = jnp.bfloat16
gelu_scale = math.sqrt(2.0 / math.pi)

D_BLK = 1536
PIECE = 192
PAIR = 384
IMG = 256
N_IMG = 8
FFB = 384
HALF = 192
N_SEM = 240


def dot(a, b):
    return jnp.dot(a, b, preferred_element_type=F32)


def dot_t(a, b):
    return lax.dot_general(a, b, (((1,), (1,)), ((), ())), preferred_element_type=F32)


def gelu_parts(gated):
    tanh_arg = gelu_scale * (gated + 0.044715 * gated * gated * gated)
    tangent = jnp.tanh(tanh_arg)
    result_value = 0.5 * gated * (1.0 + tangent)
    derivative = 0.5 * (1.0 + tangent) + 0.5 * gated * (1.0 - tangent * tangent) * gelu_scale * (
        1.0 + 3.0 * 0.044715 * gated * gated
    )
    return (result_value, derivative)


def kernel(
    tok, cot, member, in_fast, out_fast, hidden_fast, mid_fast, wu, wd,
    lo, ug, dg, fin_in, fin_out, fin_mid, fin_hid,
    gx, xn, gc, dc, eye, tab_f, tab_own, hm_col, tabs, tabt, own_col, sel, selm, st_own, st_xl, st_y, stats, col,
    pa, p_send, p_recv, h_send, h_recv, hid, upc,
    rf, rv, ruf, ru, rl, fb, bo_in,
    in_acc, in_recv, y_in, y_out, s_send, s_recv, mh_own, mh_all, ss, rs,
):
    h, c, y, x, l = [lax.axis_index(a) for a in AXES]
    here = dict(h=h, c=c, y=y, x=x, l=l)
    dp = 2 * h + c

    def at(**off):
        pos = dict(here)
        for axis, step in off.items():
            pos[axis] = lax.rem(pos[axis] + (step + SIZES[axis]), SIZES[axis])
        return tuple(pos[a] for a in AXES)

    partner = (y // 2, lax.rem(y, 2), dp, x, l)
    is_self = y == dp
    dp_parts = [at(c=1), at(h=1), at(h=1, c=1)]
    xl_parts = [(dx, dl) for dx in (0, 1, 2, 3) for dl in (0, 1) if dx or dl]
    y_parts = [1, 2, 3]

    counter = [0]
    sends = []

    def start(src, dst, dev):
        i = counter[0]
        counter[0] += 1
        copy = pltpu.make_async_remote_copy(
            src_ref=src, dst_ref=dst, send_sem=ss.at[i], recv_sem=rs.at[i],
            device_id=dev, device_id_type=MESH,
        )
        copy.start()
        sends.append(copy.wait_send)
        return copy

    def start_swap(src, dst):
        i = counter[0]
        counter[0] += 1
        copy = pltpu.make_async_remote_copy(
            src_ref=src, dst_ref=dst, send_sem=ss.at[i], recv_sem=rs.at[i],
            device_id=partner, device_id_type=MESH,
        )

        @pl.when(jnp.logical_not(is_self))
        def _():
            copy.start()

        @pl.when(is_self)
        def _():
            pltpu.make_async_copy(src, dst, rs.at[i]).start()

        def wait_send():
            @pl.when(jnp.logical_not(is_self))
            def _():
                copy.wait_send()

        sends.append(wait_send)
        return copy

    def drain(waits):
        for wait in waits:
            wait()
        waits.clear()

    bar = pltpu.get_barrier_semaphore()
    greet = dp_parts + [at(x=dx, l=dl) for dx, dl in xl_parts] + [at(y=dy) for dy in y_parts]
    for dev in greet:
        pl.semaphore_signal(bar, inc=1, device_id=dev, device_id_type=MESH)

    @pl.when(jnp.logical_not(is_self))
    def _():
        pl.semaphore_signal(bar, inc=1, device_id=partner, device_id_type=MESH)

    member_row = lax.broadcasted_iota(jnp.int32, (16, IMG), 0)
    for i in (0, 1):
        for t in (0, 1):
            sel[2 * dp + i, t] = jnp.where(member_row == member[i] + 8 * t, 1.0, 0.0).astype(BF16)
    tab_f[...] = jnp.zeros((16, FFB), F32)
    tab_f[0:4, 0:PIECE] = in_fast[...].astype(F32)
    tab_f[8:12, 0:PIECE] = out_fast[...].astype(F32)
    tab_own[...] = tab_f[:, 0:IMG].astype(BF16)

    pl.semaphore_wait(bar, jnp.where(is_self, len(greet), len(greet) + 1))

    own_piece = 2 * x + l
    own_rows = pl.ds(pl.multiple_of(PIECE * own_piece, PIECE), PIECE)

    lanes = [pl.ds(0, IMG), pl.ds(IMG, IMG)]
    swap_x = [start_swap(tok.at[:, lanes[j]], gx.at[2 * dp + j, own_rows]) for j in (0, 1)]
    swap_tab = start_swap(tab_own, tabs.at[own_piece])
    sel_mine = sel.at[pl.ds(2 * dp, 2)]
    sel_copies = [start(sel_mine, sel_mine, dev) for dev in dp_parts]

    def image(j, dy):
        return 2 * lax.rem(y + (dy + 4), 4) + j

    def chunk(ref, j, du, dv, q=None):
        dy, dx = (dv, du) if j == 0 else (du, dv)
        row = PAIR * lax.rem(x + (dx + 4), 4)
        size = PAIR
        if q is not None:
            row, size = row + PIECE * q, PIECE
        return ref.at[image(j, dy), pl.ds(pl.multiple_of(row, PIECE), size)]

    def u_dev(j, step):
        return at(x=step) if j == 0 else at(y=step)

    def v_dev(j, step):
        return at(y=step) if j == 0 else at(x=step)

    both = (0, 1)

    def gather(buf, swaps, mate):
        r = [dict(), dict()]

        def u_send(j, du, q, step, name):
            piece = chunk(buf, j, du, 0, q)
            r[j][name] = start(piece, piece, u_dev(j, step))

        def v_send(j, du, dv, step, name):
            part = chunk(buf, j, du, dv)
            r[j][name] = start(part, part, v_dev(j, step))

        def own_send(j, dv, step, name):
            piece = chunk(buf, j, 0, dv, l)
            r[j][name] = start(piece, piece, v_dev(j, step))

        def mate_send(j, dv, name):
            piece = chunk(buf, j, 0, dv, l)
            r[j][name] = start(piece, piece, at(l=1))

        for j in both:
            swaps[j].wait_recv()
            mate_send(j, 0, "l")
            u_send(j, 0, l, 1, "-own")
            u_send(j, 0, l, -1, "+own")
            if mate:
                own_send(j, 0, 1, "v-0")
                own_send(j, 0, -1, "v+0")
        yield
        for j in both:
            r[j]["l"].wait_recv()
            u_send(j, 0, 1 - l, 1, "-oth")
            u_send(j, 0, 1 - l, -1, "+oth")
        for j in both:
            r[j]["-own"].wait_recv()
            u_send(j, -1, l, 1, "fwd-")
        for j in both:
            if mate:
                r[j]["v-0"].wait_recv()
                own_send(j, -1, 1, "w-0")
                mate_send(j, -1, "m-0")
                r[j]["v+0"].wait_recv()
                mate_send(j, 1, "m+0")
            else:
                v_send(j, 0, 0, 1, "v-0")
                v_send(j, 0, 0, -1, "v+0")
        yield
        for j in both:
            r[j]["+own"].wait_recv()
            r[j]["+oth"].wait_recv()
            u_send(j, 1, 1 - l, -1, "fwd+")
            v_send(j, 1, 0, 1, "v-1")
            v_send(j, 1, 0, -1, "v+1")
            r[j]["-oth"].wait_recv()
            v_send(j, -1, 0, 1, "v-m")
            v_send(j, -1, 0, -1, "v+m")
        yield
        for j in both:
            r[j]["fwd-"].wait_recv()
            r[j]["fwd+"].wait_recv()
            v_send(j, 2, 0, 1, "v-2")
            v_send(j, 2, 0, -1, "v+2")
        for j in both:
            if mate:
                r[j]["w-0"].wait_recv()
                mate_send(j, 2, "m2")
        yield
        for j in both:
            if not mate:
                r[j]["v-0"].wait_recv()
                v_send(j, 0, -1, 1, "w-0")
            r[j]["v+1"].wait_recv()
            v_send(j, 1, 1, -1, "w+1")
            r[j]["v-m"].wait_recv()
            v_send(j, -1, -1, 1, "w-m")
        yield
        for j in both:
            r[j]["v+2"].wait_recv()
            v_send(j, 2, 1, -1, "w+2")
        for j in both:
            if mate:
                r[j]["m-0"].wait_recv()
                r[j]["m+0"].wait_recv()
            else:
                r[j]["v+0"].wait_recv()
        last_own = "m2" if mate else "w-0"
        r[1][last_own].wait_recv()
        yield
        for name in ("v+m", "v-1", "v-2"):
            for j in both:
                r[j][name].wait_recv()
        r[0][last_own].wait_recv()
        yield
        for name in ("w+1", "w-m", "w+2"):
            for j in both:
                r[j][name].wait_recv()
        yield

    def run(gen, steps=1000):
        for _ in range(steps):
            if next(gen, "end") == "end":
                return

    first = [image(0, 0)]
    second = [image(1, 0), image(0, -1), image(0, 1)]
    third = [image(1, -1), image(1, 1), image(0, 2), image(1, 2)]
    order = first + second + third

    run_x = gather(gx, swap_x, True)

    stat_row = lax.broadcasted_iota(jnp.int32, (8, IMG), 0)

    def two_rows(first_row, second_row):
        return jnp.where(stat_row == 0, first_row, jnp.where(stat_row == 1, second_row, 0.0))

    def combine(parts, count):
        mean = sum(p[0:1] for p in parts) * (1.0 / len(parts))
        dev2 = sum(p[1:2] for p in parts)
        for p in parts:
            gap = p[0:1] - mean
            dev2 = dev2 + count * (gap * gap)
        return mean, dev2

    for j in both:
        values = tok[:, lanes[j]].astype(F32)
        mean = jnp.sum(values, axis=0, keepdims=True) * (1.0 / PIECE)
        gap = values - mean
        st_own[j] = two_rows(mean, jnp.sum(gap * gap, axis=0, keepdims=True))
    st_copies = [
        start(st_own, st_xl.at[i], at(x=dx, l=dl)) for i, (dx, dl) in enumerate(xl_parts)
    ]
    run(run_x, 1)

    swap_tab.wait_recv()
    tab_copies = [
        start(tabs.at[own_piece], tabs.at[own_piece], at(x=dx, l=dl)) for dx, dl in xl_parts
    ]
    for copy in st_copies:
        copy.wait_recv()
    for j in both:
        st_y[y, j] = two_rows(
            *combine([st_own[j]] + [st_xl[i, j] for i in range(7)], float(PIECE))
        )
    st_copies = [start(st_y.at[y], st_y.at[y], at(y=dy)) for dy in y_parts]
    run(run_x, 1)
    swap_c = [start_swap(cot.at[:, lanes[j]], gc.at[2 * dp + j, own_rows]) for j in (0, 1)]
    run_c = gather(gc, swap_c, False)
    ident = lax.broadcasted_iota(jnp.int32, (FFB, FFB), 0) == lax.broadcasted_iota(
        jnp.int32, (FFB, FFB), 1
    )
    eye[...] = jnp.where(ident, 1.0, 0.0).astype(BF16)
    run(run_x, 1)
    for copy in st_copies:
        copy.wait_recv()
    for j in both:
        mean, dev2 = combine([st_y[k, j] for k in range(4)], float(D_BLK))
        stats[2 * dp + j] = two_rows(mean, lax.rsqrt(dev2 / (4 * D_BLK) + 1e-06))
    stat_mine = stats.at[pl.ds(2 * dp, 2)]
    stat_copies = [start(stat_mine, stat_mine, dev) for dev in dp_parts]
    own_col[...] = dot_t(eye[:PIECE, :IMG], tab_own[...]).astype(BF16)
    tab_f[0:4, :] = hidden_fast[...].astype(F32)
    tab_f[8:12, :] = mid_fast[...].astype(F32)
    hm_col[...] = dot_t(eye[...], tab_f[...].astype(BF16)).astype(BF16)
    col[...] = jnp.zeros((D_BLK, 128), F32)
    run(run_x, 1)
    for copy in sel_copies + stat_copies:
        copy.wait_recv()
    for copy in tab_copies:
        copy.wait_recv()
    for p in range(8):
        tabt[p * PIECE : (p + 1) * PIECE, :] = dot_t(eye[:PIECE, :IMG], tabs[p]).astype(BF16)
    lane = lax.broadcasted_iota(jnp.int32, (16, 128), 1)
    picks = jnp.zeros((16, 128), F32)
    for img in range(N_IMG):
        picks = jnp.where(lane == img, sel[img, 0][:, 0:128].astype(F32), picks)
    selm[...] = picks

    def normalise(n):
        img = order[n]
        mean, rstd = stats[img, 0:1], stats[img, 1:2]
        factor = dot(tabt[...], sel[img, 0])
        xn[img] = ((gx[img].astype(F32) - mean) * rstd * factor).astype(BF16)

    mine = pl.ds(pl.multiple_of(HALF * c, HALF), HALF)
    other = pl.ds(pl.multiple_of(HALF * (1 - c), HALF), HALF)
    core = at(c=1)
    far = at(h=1)
    near = [dict(), dict()]
    wide = [dict(), dict()]

    def partial_product(m, weight, operand, n):
        img = order[n]
        part = lax.dot_general(
            weight[...], operand[img], (((0,), (0,)), ((), ())), preferred_element_type=F32
        )
        low, high = part[0:HALF], part[HALF:FFB]
        p_send[m, img] = jnp.where(c == 0, high, low).astype(BF16)
        near[m][n] = start(p_send.at[m, img], p_recv.at[m, img], core)
        pa[m, img] = jnp.where(c == 0, low, high)

    def to_far(m, n):
        img = order[n]
        near[m][n].wait_recv()
        total = pa[m, img] + p_recv[m, img].astype(F32)
        pa[m, img] = total
        h_send[m, img] = total.astype(BF16)
        wide[m][n] = start(h_send.at[m, img], h_recv.at[m, img], far)

    hid_copies, upc_copies = {}, {}

    def finish_hidden(n):
        img = order[n]
        wide[0][n].wait_recv()
        pre_act = pa[0, img] + h_recv[0, img].astype(F32)
        pa[0, img] = pre_act
        hid_row = dot(hm_col[mine, :], sel[img, 0])
        mid_row = dot(hm_col[mine, :], sel[img, 1])
        activated, _ = gelu_parts(pre_act * hid_row)
        hid[img, mine] = (activated * mid_row).astype(BF16)
        hid_copies[n] = start(hid.at[img, mine], hid.at[img, mine], core)

    br = gx

    def branch_part(n):
        img = order[n]
        hid_copies[n].wait_recv()
        br[img] = dot(wd[...], hid[img]).astype(BF16)

    def forward(n):
        normalise(n)
        partial_product(0, wu, xn, n)

    def backward(n):
        img = order[n]
        factor = dot(tabt[...], sel[img, 1])
        dc[img] = (gc[img].astype(F32) * factor).astype(BF16)
        partial_product(1, wd, dc, n)

    def each(step, *numbers):
        for n in numbers:
            step(n)

    forward(0)
    run(run_x, 1)
    to_far(0, 0)
    run(run_x, 1)
    forward(1)
    run(run_c, 1)
    to_far(0, 1)
    run(run_x, 1)
    forward(2)
    forward(3)
    to_far(0, 2)
    to_far(0, 3)
    run(run_x, 1)
    x_sends = list(sends)
    sends.clear()
    run(run_c, 1)
    forward(4)
    forward(5)
    to_far(0, 4)
    forward(6)
    to_far(0, 5)
    forward(7)
    to_far(0, 6)
    to_far(0, 7)
    run(run_c, 1)
    each(finish_hidden, 0, 1, 2, 3)
    run(run_c, 1)
    drain(x_sends)
    each(branch_part, 0, 1, 2, 3)
    finish_hidden(4)
    run(run_c, 1)
    finish_hidden(5)
    branch_part(4)
    finish_hidden(6)
    branch_part(5)
    run(run_c, 1)
    finish_hidden(7)
    branch_part(6)
    branch_part(7)

    up, down = (0, -1), (1, 2)
    slot = {0: 0, -1: 1, 1: 2, 2: 3}

    def add_into(dst, *terms):
        total = dst[...].astype(F32)
        for term in terms:
            total = total + term[...].astype(F32)
        dst[...] = total.astype(BF16)

    finals = []

    def scatter():
        r = [dict(), dict()]
        for j in both:
            for i in (0, 1):
                r[j]["f+", up[i]] = start(chunk(br, j, up[i], 2), rf.at[j, 0, i], v_dev(j, 1))
                r[j]["f-", down[i]] = start(chunk(br, j, down[i], 2), rf.at[j, 1, i], v_dev(j, -1))
        for j in both:
            for k in (2, 1):
                r[j]["d+", k] = start(chunk(br, j, k, 1), rv.at[j, 0, slot[k]], v_dev(j, 1))
            for k in (-1, 0):
                r[j]["d-", k] = start(chunk(br, j, k, -1), rv.at[j, 1, slot[k]], v_dev(j, -1))
        yield
        for i in (1, 0):
            for j in both:
                r[j]["f+", up[i]].wait_recv()
                part = chunk(br, j, up[i], 1)
                add_into(part, rf.at[j, 0, i])
                r[j]["d+", up[i]] = start(part, rv.at[j, 0, slot[up[i]]], v_dev(j, 1))
                r[j]["f-", down[i]].wait_recv()
                part = chunk(br, j, down[i], -1)
                add_into(part, rf.at[j, 1, i])
                r[j]["d-", down[i]] = start(part, rv.at[j, 1, slot[down[i]]], v_dev(j, -1))
            yield

        def total(j, k):
            r[j]["d+", k].wait_recv()
            r[j]["d-", k].wait_recv()
            part = chunk(br, j, k, 0)
            add_into(part, rv.at[j, 0, slot[k]], rv.at[j, 1, slot[k]])

        for j in both:
            total(j, 2)
            r[j]["uf+"] = start(chunk(br, j, 2, 0, 0), ruf.at[j, 0], u_dev(j, 1))
            r[j]["uf-"] = start(chunk(br, j, 2, 0, 1), ruf.at[j, 1], u_dev(j, -1))
        yield
        low, high = pl.ds(0, PIECE), pl.ds(PIECE, PIECE)
        for j in both:
            total(j, -1)
            r[j]["u-0"] = start(chunk(br, j, -1, 0, 0), ru.at[j, 1, low], u_dev(j, -1))
        for j in both:
            total(j, 1)
            r[j]["u+1"] = start(chunk(br, j, 1, 0, 1), ru.at[j, 0, high], u_dev(j, 1))
        yield
        for j in both:
            r[j]["uf+"].wait_recv()
            part = chunk(br, j, 1, 0, 0)
            add_into(part, ruf.at[j, 0])
            r[j]["u+0"] = start(part, ru.at[j, 0, low], u_dev(j, 1))
            r[j]["uf-"].wait_recv()
            part = chunk(br, j, -1, 0, 1)
            add_into(part, ruf.at[j, 1])
            r[j]["u-1"] = start(part, ru.at[j, 1, high], u_dev(j, -1))
        for j in both:
            total(j, 0)
        yield
        for j in both:
            for name in ("u+1", "u+0", "u-0", "u-1"):
                r[j][name].wait_recv()
            add_into(chunk(br, j, 0, 0), ru.at[j, 0], ru.at[j, 1])
            r[j]["l"] = start(chunk(br, j, 0, 0, 1 - l), rl.at[j], at(l=1))
        yield
        for j in both:
            r[j]["l"].wait_recv()
            piece = chunk(br, j, 0, 0, l)[...].astype(F32) + rl[j].astype(F32)
            fb[j] = piece.astype(BF16)
            finals.append(start_swap(fb.at[j], bo_in.at[j]))
        yield

    run_s = scatter()
    run(run_s, 1)

    mh_own[...] = jnp.zeros((32, IMG), F32)

    def finish_cot(n):
        img = order[n]
        wide[1][n].wait_recv()
        grad_act = pa[1, img] + h_recv[1, img].astype(F32)
        pre_act = pa[0, img]
        hid_row = dot(hm_col[mine, :], sel[img, 0])
        mid_row = dot(hm_col[mine, :], sel[img, 1])
        activated, derivative = gelu_parts(pre_act * hid_row)
        grad_gated = grad_act * mid_row * derivative
        upc[img, mine] = (grad_gated * hid_row).astype(BF16)
        upc_copies[n] = start(upc.at[img, mine], upc.at[img, mine], core)
        pick = sel[img, 0]
        mh_own[0:16, 0:HALF] += dot_t(pick, (activated * grad_act).astype(BF16))
        mh_own[16:32, 0:HALF] += dot_t(pick, (pre_act * grad_gated).astype(BF16))

    def down_rows(k):
        rows = pl.ds(k * PAIR, PAIR)
        acc = dot_t(dc[0, rows], hid[0])
        for img in range(1, 8):
            acc = acc + dot_t(dc[img, rows], hid[img])
        dg[rows, :] = acc.astype(BF16)

    def up_rows(k):
        rows = pl.ds(k * PAIR, PAIR)
        weight = wu[rows, :].astype(F32)
        acc = jnp.zeros((PAIR, FFB), F32)
        for img in range(8):
            part = dot_t(xn[img, rows], upc[img])
            acc = acc + part
            col[rows, img : img + 1] = jnp.sum(part * weight, axis=1, keepdims=True)
        ug[rows, :] = acc.astype(BF16)

    backward(0)
    backward(1)
    to_far(1, 0)
    run(run_c, 1)
    backward(2)
    to_far(1, 1)
    backward(3)
    to_far(1, 2)
    run(run_c, 1)
    for n in (4, 5, 6, 7):
        backward(n)
        to_far(1, n - 1)
    to_far(1, 7)
    run(run_s, 1)
    each(finish_cot, 0, 1)
    run(run_s, 1)
    each(finish_cot, 2, 3)
    down_rows(0)
    finish_cot(4)
    down_rows(1)
    run(run_s, 1)
    each(finish_cot, 5, 6, 7)
    mh_all[dp] = mh_own[...]
    mh_copies = [start(mh_own, mh_all.at[dp], dev) for dev in dp_parts]
    down_rows(2)
    run(run_s, 1)
    down_rows(3)
    for n in range(8):
        upc_copies[n].wait_recv()
    up_rows(0)
    run(run_s, 1)
    up_rows(1)
    run(run_s, 1)
    each(up_rows, 2, 3)

    in_acc[...] = jnp.zeros((8, 16, IMG), F32)
    for p in range(8):
        in_acc[p, :, 0:PIECE] = lax.dot_general(
            selm[...], col[p * PIECE : (p + 1) * PIECE, :], (((1,), (1,)), ((), ())),
            precision=lax.Precision.HIGHEST, preferred_element_type=F32,
        )
    in_copies = []
    for i, (dx, dl) in enumerate(xl_parts):
        p_to = 2 * lax.rem(x + dx, 4) + lax.rem(l + dl, 2)
        in_copies.append(start(in_acc.at[p_to], in_recv.at[i], at(x=dx, l=dl)))
    for copy in in_copies:
        copy.wait_recv()
    total_in = in_acc[own_piece]
    for i in range(7):
        total_in = total_in + in_recv[i]
    y_in[y] = total_in
    y_in_copies = [start(y_in.at[y], y_in.at[y], at(y=dy)) for dy in y_parts]
    run(run_s)

    out_total = jnp.zeros((16, PIECE), F32)
    for j in both:
        prod = gc[2 * y + j, own_rows].astype(F32) * fb[j].astype(F32)
        out_total = out_total + dot_t(sel[2 * y + j, 0], prod.astype(BF16))
    y_out[y] = jnp.zeros((16, IMG), F32)
    y_out[y, :, 0:PIECE] = out_total
    y_out_copies = [start(y_out.at[y], y_out.at[y], at(y=dy)) for dy in y_parts]
    for copy in y_in_copies + y_out_copies:
        copy.wait_recv()
    s_send[0] = (y_in[0] + y_in[1]) + (y_in[2] + y_in[3])
    s_send[1] = (y_out[0] + y_out[1]) + (y_out[2] + y_out[3])
    last = start_swap(s_send, s_recv)
    for copy in mh_copies:
        copy.wait_recv()
    fin_mid[...] = jnp.concatenate([mh_all[0, 0:4, 0:HALF], mh_all[1, 0:4, 0:HALF]], axis=1)
    fin_hid[...] = jnp.concatenate([mh_all[0, 16:20, 0:HALF], mh_all[1, 16:20, 0:HALF]], axis=1)
    for j in both:
        finals[j].wait_recv()
        factor = dot(own_col[...], sel[2 * dp + j, 1])
        lo[:, lanes[j]] = (
            tok[:, lanes[j]].astype(F32) + bo_in[j].astype(F32) * factor
        ).astype(BF16)
    last.wait_recv()
    fin_in[...] = s_recv[0, 0:4, 0:PIECE] / in_fast[...].astype(F32)
    fin_out[...] = s_recv[1, 0:4, 0:PIECE]
    drain(sends)


def widen(ug, dg, lo, *small):
    def copy(*refs):
        n = len(refs) // 2
        for src, dst in zip(refs[:n], refs[n:]):
            dst[...] = src[...].astype(dst.dtype)

    def spec(a, split):
        if split:
            return pl.BlockSpec((a.shape[0] // 4, a.shape[1]), lambda i: (i, 0))
        return pl.BlockSpec(a.shape, lambda i: (0, 0))

    arrays = (ug, dg, lo) + small
    specs = [spec(a, n < 2) for n, a in enumerate(arrays)]
    return pl.pallas_call(
        copy,
        grid=(4,),
        in_specs=specs,
        out_specs=specs,
        out_shape=[
            jax.ShapeDtypeStruct(a.shape, F32 if n < 2 else a.dtype)
            for n, a in enumerate(arrays)
        ],
    )(*arrays)


def exchange(*arrays):
    vmem = pl.BlockSpec(memory_space=pltpu.VMEM)
    smem = pl.BlockSpec(memory_space=pltpu.SMEM)
    out_shape = [
        jax.ShapeDtypeStruct((PIECE, 2 * IMG), BF16),
        jax.ShapeDtypeStruct((D_BLK, FFB), BF16),
        jax.ShapeDtypeStruct((D_BLK, FFB), BF16),
        jax.ShapeDtypeStruct((4, PIECE), F32),
        jax.ShapeDtypeStruct((4, PIECE), F32),
        jax.ShapeDtypeStruct((4, FFB), F32),
        jax.ShapeDtypeStruct((4, FFB), F32),
    ]
    scratch = [
        ((N_IMG, D_BLK, IMG), BF16),
        ((N_IMG, D_BLK, IMG), BF16),
        ((N_IMG, D_BLK, IMG), BF16),
        ((N_IMG, D_BLK, IMG), BF16),
        ((FFB, FFB), BF16),
        ((16, FFB), F32),
        ((16, IMG), BF16),
        ((FFB, 16), BF16),
        ((8, 16, IMG), BF16),
        ((D_BLK, 16), BF16),
        ((PIECE, 16), BF16),
        ((N_IMG, 2, 16, IMG), BF16),
        ((16, 128), F32),
        ((2, 8, IMG), F32),
        ((7, 2, 8, IMG), F32),
        ((4, 2, 8, IMG), F32),
        ((N_IMG, 8, IMG), F32),
        ((D_BLK, 128), F32),
        ((2, N_IMG, HALF, IMG), F32),
        ((2, N_IMG, HALF, IMG), BF16),
        ((2, N_IMG, HALF, IMG), BF16),
        ((2, N_IMG, HALF, IMG), BF16),
        ((2, N_IMG, HALF, IMG), BF16),
        ((N_IMG, FFB, IMG), BF16),
        ((N_IMG, FFB, IMG), BF16),
        ((2, 2, 2, PAIR, IMG), BF16),
        ((2, 2, 4, PAIR, IMG), BF16),
        ((2, 2, PIECE, IMG), BF16),
        ((2, 2, PAIR, IMG), BF16),
        ((2, PIECE, IMG), BF16),
        ((2, PIECE, IMG), BF16),
        ((2, PIECE, IMG), BF16),
        ((8, 16, IMG), F32),
        ((7, 16, IMG), F32),
        ((4, 16, IMG), F32),
        ((4, 16, IMG), F32),
        ((2, 16, IMG), F32),
        ((2, 16, IMG), F32),
        ((32, IMG), F32),
        ((4, 32, IMG), F32),
    ]
    return pl.pallas_call(
        kernel,
        out_shape=out_shape,
        in_specs=[vmem, vmem, smem] + [vmem] * 6,
        out_specs=[vmem] * 7,
        scratch_shapes=[pltpu.VMEM(s, d) for s, d in scratch]
        + [pltpu.SemaphoreType.DMA((N_SEM,)), pltpu.SemaphoreType.DMA((N_SEM,))],
        compiler_params=pltpu.CompilerParams(
            collective_id=0, has_side_effects=True, vmem_limit_bytes=62 * 1024 * 1024
        ),
        cost_estimate=pl.CostEstimate(
            flops=14_500_000_000, bytes_accessed=12_000_000, transcendentals=1_600_000
        ),
    )(*arrays)


def body(
    tokens, member, up_weight, down_weight, in_fast, hidden_fast, mid_fast, out_fast, cotangent
):
    lo, ug, dg, in_grad, out_grad, mid_grad, hidden_grad = exchange(
        tokens.T, cotangent.T, member, in_fast, out_fast, hidden_fast, mid_fast,
        up_weight, down_weight,
    )
    ug, dg, lo, in_grad, out_grad, mid_grad, hidden_grad = widen(
        ug, dg, lo, in_grad, out_grad, mid_grad, hidden_grad
    )
    return (lo.T, ug, dg, in_grad, hidden_grad, mid_grad, out_grad)


def solution(mesh):
    grid = Mesh(mesh.devices.reshape([SIZES[a] for a in AXES]), AXES)
    dp, mp = ("h", "c"), ("y", "x", "l")
    in_specs = (
        P(dp, mp),
        P(dp),
        P(dp, mp),
        P(dp, mp),
        P(None, mp),
        P(None, mp),
        P(None, mp),
        P(None, mp),
        P(dp, mp),
    )
    out_specs = (
        P(dp, mp),
        P(dp, mp),
        P(dp, mp),
        P(None, mp),
        P(None, mp),
        P(None, mp),
        P(None, mp),
    )
    return jax.shard_map(body, mesh=grid, in_specs=in_specs, out_specs=out_specs, check_vma=False)
```

```python
import math

import jax
import jax.numpy as jnp
from jax import lax
from jax.experimental import pallas as pl
from jax.experimental.pallas import tpu as pltpu
from jax.sharding import Mesh
from jax.sharding import PartitionSpec as P

AXES = ("h", "c", "y", "x", "l")
SIZES = dict(h=2, c=2, y=4, x=4, l=2)
MESH = pl.DeviceIdType.MESH
F32 = jnp.float32
BF16 = jnp.bfloat16
gelu_scale = math.sqrt(2.0 / math.pi)

D_BLK = 1536
PIECE = 192
PAIR = 384
IMG = 256
N_IMG = 8
FFB = 384
HALF = 192
N_SEM = 240


def dot(a, b):
    return jnp.dot(a, b, preferred_element_type=F32)


def dot_t(a, b):
    return lax.dot_general(a, b, (((1,), (1,)), ((), ())), preferred_element_type=F32)


def gelu_parts(gated):
    tanh_arg = gelu_scale * (gated + 0.044715 * gated * gated * gated)
    tangent = jnp.tanh(tanh_arg)
    result_value = 0.5 * gated * (1.0 + tangent)
    derivative = 0.5 * (1.0 + tangent) + 0.5 * gated * (1.0 - tangent * tangent) * gelu_scale * (
        1.0 + 3.0 * 0.044715 * gated * gated
    )
    return (result_value, derivative)


def kernel(
    tok, cot, member, in_fast, out_fast, hidden_fast, mid_fast, wu, wd,
    lo, ug, dg, fin_in, fin_out, fin_mid, fin_hid,
    gx, xn, gc, dc, eye, tab_f, tab_own, hm_col, tabs, tabt, own_col, sel, selm, st_own, st_xl, st_y, stats, col,
    pa, p_send, p_recv, h_send, h_recv, hid, upc,
    rf, rv, ruf, ru, rl, fb, bo_in,
    in_acc, in_recv, y_in, y_out, s_send, s_recv, mh_own, mh_all, ss, rs,
):
    h, c, y, x, l = [lax.axis_index(a) for a in AXES]
    here = dict(h=h, c=c, y=y, x=x, l=l)
    dp = 2 * h + c

    def at(**off):
        pos = dict(here)
        for axis, step in off.items():
            pos[axis] = lax.rem(pos[axis] + (step + SIZES[axis]), SIZES[axis])
        return tuple(pos[a] for a in AXES)

    partner = (y // 2, lax.rem(y, 2), dp, x, l)
    is_self = y == dp
    dp_parts = [at(c=1), at(h=1), at(h=1, c=1)]
    xl_parts = [(dx, dl) for dx in (0, 1, 2, 3) for dl in (0, 1) if dx or dl]
    y_parts = [1, 2, 3]

    counter = [0]
    sends = []

    def start(src, dst, dev):
        i = counter[0]
        counter[0] += 1
        copy = pltpu.make_async_remote_copy(
            src_ref=src, dst_ref=dst, send_sem=ss.at[i], recv_sem=rs.at[i],
            device_id=dev, device_id_type=MESH,
        )
        copy.start()
        sends.append(copy.wait_send)
        return copy

    def start_swap(src, dst):
        i = counter[0]
        counter[0] += 1
        copy = pltpu.make_async_remote_copy(
            src_ref=src, dst_ref=dst, send_sem=ss.at[i], recv_sem=rs.at[i],
            device_id=partner, device_id_type=MESH,
        )

        @pl.when(jnp.logical_not(is_self))
        def _():
            copy.start()

        @pl.when(is_self)
        def _():
            pltpu.make_async_copy(src, dst, rs.at[i]).start()

        def wait_send():
            @pl.when(jnp.logical_not(is_self))
            def _():
                copy.wait_send()

        sends.append(wait_send)
        return copy

    def drain(waits):
        for wait in waits:
            wait()
        waits.clear()

    bar = pltpu.get_barrier_semaphore()
    greet = dp_parts + [at(x=dx, l=dl) for dx, dl in xl_parts] + [at(y=dy) for dy in y_parts]
    for dev in greet:
        pl.semaphore_signal(bar, inc=1, device_id=dev, device_id_type=MESH)

    @pl.when(jnp.logical_not(is_self))
    def _():
        pl.semaphore_signal(bar, inc=1, device_id=partner, device_id_type=MESH)

    member_row = lax.broadcasted_iota(jnp.int32, (16, IMG), 0)
    for i in (0, 1):
        for t in (0, 1):
            sel[2 * dp + i, t] = jnp.where(member_row == member[i] + 8 * t, 1.0, 0.0).astype(BF16)
    tab_f[...] = jnp.zeros((16, FFB), F32)
    tab_f[0:4, 0:PIECE] = in_fast[...].astype(F32)
    tab_f[8:12, 0:PIECE] = out_fast[...].astype(F32)
    tab_own[...] = tab_f[:, 0:IMG].astype(BF16)

    pl.semaphore_wait(bar, jnp.where(is_self, len(greet), len(greet) + 1))

    own_piece = 2 * x + l
    own_rows = pl.ds(pl.multiple_of(PIECE * own_piece, PIECE), PIECE)

    lanes = [pl.ds(0, IMG), pl.ds(IMG, IMG)]
    swap_x = [start_swap(tok.at[:, lanes[j]], gx.at[2 * dp + j, own_rows]) for j in (0, 1)]
    swap_tab = start_swap(tab_own, tabs.at[own_piece])
    sel_mine = sel.at[pl.ds(2 * dp, 2)]
    sel_copies = [start(sel_mine, sel_mine, dev) for dev in dp_parts]

    def image(j, dy):
        return 2 * lax.rem(y + (dy + 4), 4) + j

    def chunk(ref, j, du, dv, q=None):
        dy, dx = (dv, du) if j == 0 else (du, dv)
        row = PAIR * lax.rem(x + (dx + 4), 4)
        size = PAIR
        if q is not None:
            row, size = row + PIECE * q, PIECE
        return ref.at[image(j, dy), pl.ds(pl.multiple_of(row, PIECE), size)]

    def u_dev(j, step):
        return at(x=step) if j == 0 else at(y=step)

    def v_dev(j, step):
        return at(y=step) if j == 0 else at(x=step)

    both = (0, 1)

    def gather(buf, swaps, mate):
        r = [dict(), dict()]

        def u_send(j, du, q, step, name):
            piece = chunk(buf, j, du, 0, q)
            r[j][name] = start(piece, piece, u_dev(j, step))

        def v_send(j, du, dv, step, name):
            part = chunk(buf, j, du, dv)
            r[j][name] = start(part, part, v_dev(j, step))

        def own_send(j, dv, step, name):
            piece = chunk(buf, j, 0, dv, l)
            r[j][name] = start(piece, piece, v_dev(j, step))

        def mate_send(j, dv, name):
            piece = chunk(buf, j, 0, dv, l)
            r[j][name] = start(piece, piece, at(l=1))

        for j in both:
            swaps[j].wait_recv()
            mate_send(j, 0, "l")
            u_send(j, 0, l, 1, "-own")
            u_send(j, 0, l, -1, "+own")
            if mate:
                own_send(j, 0, 1, "v-0")
                own_send(j, 0, -1, "v+0")
        yield
        for j in both:
            r[j]["l"].wait_recv()
            u_send(j, 0, 1 - l, 1, "-oth")
            u_send(j, 0, 1 - l, -1, "+oth")
        for j in both:
            r[j]["-own"].wait_recv()
            u_send(j, -1, l, 1, "fwd-")
        for j in both:
            if mate:
                r[j]["v-0"].wait_recv()
                own_send(j, -1, 1, "w-0")
                mate_send(j, -1, "m-0")
                r[j]["v+0"].wait_recv()
                mate_send(j, 1, "m+0")
            else:
                v_send(j, 0, 0, 1, "v-0")
                v_send(j, 0, 0, -1, "v+0")
        yield
        for j in both:
            r[j]["+own"].wait_recv()
            r[j]["+oth"].wait_recv()
            u_send(j, 1, 1 - l, -1, "fwd+")
            v_send(j, 1, 0, 1, "v-1")
            v_send(j, 1, 0, -1, "v+1")
            r[j]["-oth"].wait_recv()
            v_send(j, -1, 0, 1, "v-m")
            v_send(j, -1, 0, -1, "v+m")
        yield
        for j in both:
            r[j]["fwd-"].wait_recv()
            r[j]["fwd+"].wait_recv()
            v_send(j, 2, 0, 1, "v-2")
            v_send(j, 2, 0, -1, "v+2")
        for j in both:
            if mate:
                r[j]["w-0"].wait_recv()
                mate_send(j, 2, "m2")
        yield
        for j in both:
            if not mate:
                r[j]["v-0"].wait_recv()
                v_send(j, 0, -1, 1, "w-0")
            r[j]["v+1"].wait_recv()
            v_send(j, 1, 1, -1, "w+1")
            r[j]["v-m"].wait_recv()
            v_send(j, -1, -1, 1, "w-m")
        yield
        for j in both:
            r[j]["v+2"].wait_recv()
            v_send(j, 2, 1, -1, "w+2")
        for j in both:
            if mate:
                r[j]["m-0"].wait_recv()
                r[j]["m+0"].wait_recv()
            else:
                r[j]["v+0"].wait_recv()
        last_own = "m2" if mate else "w-0"
        r[1][last_own].wait_recv()
        yield
        for name in ("v+m", "v-1", "v-2"):
            for j in both:
                r[j][name].wait_recv()
        r[0][last_own].wait_recv()
        yield
        for name in ("w+1", "w-m", "w+2"):
            for j in both:
                r[j][name].wait_recv()
        yield

    def run(gen, steps=1000):
        for _ in range(steps):
            if next(gen, "end") == "end":
                return

    first = [image(0, 0)]
    second = [image(1, 0), image(0, -1), image(0, 1)]
    third = [image(1, -1), image(1, 1), image(0, 2), image(1, 2)]
    order = first + second + third

    run_x = gather(gx, swap_x, True)

    stat_row = lax.broadcasted_iota(jnp.int32, (8, IMG), 0)

    def two_rows(first_row, second_row):
        return jnp.where(stat_row == 0, first_row, jnp.where(stat_row == 1, second_row, 0.0))

    def combine(parts, count):
        mean = sum(p[0:1] for p in parts) * (1.0 / len(parts))
        dev2 = sum(p[1:2] for p in parts)
        for p in parts:
            gap = p[0:1] - mean
            dev2 = dev2 + count * (gap * gap)
        return mean, dev2

    for j in both:
        values = tok[:, lanes[j]].astype(F32)
        mean = jnp.sum(values, axis=0, keepdims=True) * (1.0 / PIECE)
        gap = values - mean
        st_own[j] = two_rows(mean, jnp.sum(gap * gap, axis=0, keepdims=True))
    st_copies = [
        start(st_own, st_xl.at[i], at(x=dx, l=dl)) for i, (dx, dl) in enumerate(xl_parts)
    ]
    run(run_x, 1)

    swap_tab.wait_recv()
    tab_copies = [
        start(tabs.at[own_piece], tabs.at[own_piece], at(x=dx, l=dl)) for dx, dl in xl_parts
    ]
    for copy in st_copies:
        copy.wait_recv()
    for j in both:
        st_y[y, j] = two_rows(
            *combine([st_own[j]] + [st_xl[i, j] for i in range(7)], float(PIECE))
        )
    st_copies = [start(st_y.at[y], st_y.at[y], at(y=dy)) for dy in y_parts]
    run(run_x, 1)
    swap_c = [start_swap(cot.at[:, lanes[j]], gc.at[2 * dp + j, own_rows]) for j in (0, 1)]
    run_c = gather(gc, swap_c, False)
    ident = lax.broadcasted_iota(jnp.int32, (FFB, FFB), 0) == lax.broadcasted_iota(
        jnp.int32, (FFB, FFB), 1
    )
    eye[...] = jnp.where(ident, 1.0, 0.0).astype(BF16)
    run(run_x, 1)
    for copy in st_copies:
        copy.wait_recv()
    for j in both:
        mean, dev2 = combine([st_y[k, j] for k in range(4)], float(D_BLK))
        stats[2 * dp + j] = two_rows(mean, lax.rsqrt(dev2 / (4 * D_BLK) + 1e-06))
    stat_mine = stats.at[pl.ds(2 * dp, 2)]
    stat_copies = [start(stat_mine, stat_mine, dev) for dev in dp_parts]
    own_col[...] = dot_t(eye[:PIECE, :IMG], tab_own[...]).astype(BF16)
    tab_f[0:4, :] = hidden_fast[...].astype(F32)
    tab_f[8:12, :] = mid_fast[...].astype(F32)
    hm_col[...] = dot_t(eye[...], tab_f[...].astype(BF16)).astype(BF16)
    col[...] = jnp.zeros((D_BLK, 128), F32)
    run(run_x, 1)
    for copy in sel_copies + stat_copies:
        copy.wait_recv()
    for copy in tab_copies:
        copy.wait_recv()
    for p in range(8):
        tabt[p * PIECE : (p + 1) * PIECE, :] = dot_t(eye[:PIECE, :IMG], tabs[p]).astype(BF16)
    lane = lax.broadcasted_iota(jnp.int32, (16, 128), 1)
    picks = jnp.zeros((16, 128), F32)
    for img in range(N_IMG):
        picks = jnp.where(lane == img, sel[img, 0][:, 0:128].astype(F32), picks)
    selm[...] = picks

    def normalise(n):
        img = order[n]
        mean, rstd = stats[img, 0:1], stats[img, 1:2]
        factor = dot(tabt[...], sel[img, 0])
        xn[img] = ((gx[img].astype(F32) - mean) * rstd * factor).astype(BF16)

    mine = pl.ds(pl.multiple_of(HALF * c, HALF), HALF)
    other = pl.ds(pl.multiple_of(HALF * (1 - c), HALF), HALF)
    core = at(c=1)
    far = at(h=1)
    near = [dict(), dict()]
    wide = [dict(), dict()]

    def partial_product(m, weight, operand, n):
        img = order[n]
        part = lax.dot_general(
            weight[...], operand[img], (((0,), (0,)), ((), ())), preferred_element_type=F32
        )
        low, high = part[0:HALF], part[HALF:FFB]
        p_send[m, img] = jnp.where(c == 0, high, low).astype(BF16)
        near[m][n] = start(p_send.at[m, img], p_recv.at[m, img], core)
        pa[m, img] = jnp.where(c == 0, low, high)

    def to_far(m, n):
        img = order[n]
        near[m][n].wait_recv()
        total = pa[m, img] + p_recv[m, img].astype(F32)
        pa[m, img] = total
        h_send[m, img] = total.astype(BF16)
        wide[m][n] = start(h_send.at[m, img], h_recv.at[m, img], far)

    hid_copies, upc_copies = {}, {}

    def finish_hidden(n):
        img = order[n]
        wide[0][n].wait_recv()
        pre_act = pa[0, img] + h_recv[0, img].astype(F32)
        pa[0, img] = pre_act
        hid_row = dot(hm_col[mine, :], sel[img, 0])
        mid_row = dot(hm_col[mine, :], sel[img, 1])
        activated, _ = gelu_parts(pre_act * hid_row)
        hid[img, mine] = (activated * mid_row).astype(BF16)
        hid_copies[n] = start(hid.at[img, mine], hid.at[img, mine], core)

    br = gx

    def branch_part(n):
        img = order[n]
        hid_copies[n].wait_recv()
        br[img] = dot(wd[...], hid[img]).astype(BF16)

    def forward(n):
        normalise(n)
        partial_product(0, wu, xn, n)

    def backward(n):
        img = order[n]
        factor = dot(tabt[...], sel[img, 1])
        dc[img] = (gc[img].astype(F32) * factor).astype(BF16)
        partial_product(1, wd, dc, n)

    def each(step, *numbers):
        for n in numbers:
            step(n)

    forward(0)
    run(run_x, 1)
    to_far(0, 0)
    run(run_x, 1)
    forward(1)
    run(run_c, 1)
    to_far(0, 1)
    run(run_x, 1)
    forward(2)
    forward(3)
    to_far(0, 2)
    to_far(0, 3)
    run(run_x, 1)
    x_sends = list(sends)
    sends.clear()
    run(run_c, 1)
    forward(4)
    forward(5)
    to_far(0, 4)
    forward(6)
    to_far(0, 5)
    forward(7)
    to_far(0, 6)
    to_far(0, 7)
    run(run_c, 1)
    each(finish_hidden, 0, 1, 2, 3)
    run(run_c, 1)
    drain(x_sends)
    each(branch_part, 0, 1, 2, 3)
    finish_hidden(4)
    run(run_c, 1)
    finish_hidden(5)
    branch_part(4)
    finish_hidden(6)
    branch_part(5)
    run(run_c, 1)
    finish_hidden(7)
    branch_part(6)
    branch_part(7)

    up, down = (0, -1), (1, 2)
    slot = {0: 0, -1: 1, 1: 2, 2: 3}

    def add_into(dst, *terms):
        total = dst[...].astype(F32)
        for term in terms:
            total = total + term[...].astype(F32)
        dst[...] = total.astype(BF16)

    finals = []

    def scatter():
        r = [dict(), dict()]
        for j in both:
            for i in (0, 1):
                r[j]["f+", up[i]] = start(chunk(br, j, up[i], 2), rf.at[j, 0, i], v_dev(j, 1))
                r[j]["f-", down[i]] = start(chunk(br, j, down[i], 2), rf.at[j, 1, i], v_dev(j, -1))
        for j in both:
            for k in (2, 1):
                r[j]["d+", k] = start(chunk(br, j, k, 1), rv.at[j, 0, slot[k]], v_dev(j, 1))
            for k in (-1, 0):
                r[j]["d-", k] = start(chunk(br, j, k, -1), rv.at[j, 1, slot[k]], v_dev(j, -1))
        yield
        for i in (1, 0):
            for j in both:
                r[j]["f+", up[i]].wait_recv()
                part = chunk(br, j, up[i], 1)
                add_into(part, rf.at[j, 0, i])
                r[j]["d+", up[i]] = start(part, rv.at[j, 0, slot[up[i]]], v_dev(j, 1))
                r[j]["f-", down[i]].wait_recv()
                part = chunk(br, j, down[i], -1)
                add_into(part, rf.at[j, 1, i])
                r[j]["d-", down[i]] = start(part, rv.at[j, 1, slot[down[i]]], v_dev(j, -1))
            yield

        def total(j, k):
            r[j]["d+", k].wait_recv()
            r[j]["d-", k].wait_recv()
            part = chunk(br, j, k, 0)
            add_into(part, rv.at[j, 0, slot[k]], rv.at[j, 1, slot[k]])

        for j in both:
            total(j, 2)
            r[j]["uf+"] = start(chunk(br, j, 2, 0, 0), ruf.at[j, 0], u_dev(j, 1))
            r[j]["uf-"] = start(chunk(br, j, 2, 0, 1), ruf.at[j, 1], u_dev(j, -1))
        yield
        low, high = pl.ds(0, PIECE), pl.ds(PIECE, PIECE)
        for j in both:
            total(j, -1)
            r[j]["u-0"] = start(chunk(br, j, -1, 0, 0), ru.at[j, 1, low], u_dev(j, -1))
        for j in both:
            total(j, 1)
            r[j]["u+1"] = start(chunk(br, j, 1, 0, 1), ru.at[j, 0, high], u_dev(j, 1))
        yield
        for j in both:
            r[j]["uf+"].wait_recv()
            part = chunk(br, j, 1, 0, 0)
            add_into(part, ruf.at[j, 0])
            r[j]["u+0"] = start(part, ru.at[j, 0, low], u_dev(j, 1))
            r[j]["uf-"].wait_recv()
            part = chunk(br, j, -1, 0, 1)
            add_into(part, ruf.at[j, 1])
            r[j]["u-1"] = start(part, ru.at[j, 1, high], u_dev(j, -1))
        for j in both:
            total(j, 0)
        yield
        for j in both:
            for name in ("u+1", "u+0", "u-0", "u-1"):
                r[j][name].wait_recv()
            add_into(chunk(br, j, 0, 0), ru.at[j, 0], ru.at[j, 1])
            r[j]["l"] = start(chunk(br, j, 0, 0, 1 - l), rl.at[j], at(l=1))
        yield
        for j in both:
            r[j]["l"].wait_recv()
            piece = chunk(br, j, 0, 0, l)[...].astype(F32) + rl[j].astype(F32)
            fb[j] = piece.astype(BF16)
            finals.append(start_swap(fb.at[j], bo_in.at[j]))
        yield

    run_s = scatter()
    run(run_s, 1)

    mh_own[...] = jnp.zeros((32, IMG), F32)

    def finish_cot(n):
        img = order[n]
        wide[1][n].wait_recv()
        grad_act = pa[1, img] + h_recv[1, img].astype(F32)
        pre_act = pa[0, img]
        hid_row = dot(hm_col[mine, :], sel[img, 0])
        mid_row = dot(hm_col[mine, :], sel[img, 1])
        activated, derivative = gelu_parts(pre_act * hid_row)
        grad_gated = grad_act * mid_row * derivative
        upc[img, mine] = (grad_gated * hid_row).astype(BF16)
        upc_copies[n] = start(upc.at[img, mine], upc.at[img, mine], core)
        pick = sel[img, 0]
        mh_own[0:16, 0:HALF] += dot_t(pick, (activated * grad_act).astype(BF16))
        mh_own[16:32, 0:HALF] += dot_t(pick, (pre_act * grad_gated).astype(BF16))

    def down_rows(k):
        rows = pl.ds(k * PAIR, PAIR)
        acc = dot_t(dc[0, rows], hid[0])
        for img in range(1, 8):
            acc = acc + dot_t(dc[img, rows], hid[img])
        dg[rows, :] = acc.astype(BF16)

    def up_rows(k):
        rows = pl.ds(k * PAIR, PAIR)
        weight = wu[rows, :].astype(F32)
        acc = jnp.zeros((PAIR, FFB), F32)
        for img in range(8):
            part = dot_t(xn[img, rows], upc[img])
            acc = acc + part
            col[rows, img : img + 1] = jnp.sum(part * weight, axis=1, keepdims=True)
        ug[rows, :] = acc.astype(BF16)

    backward(0)
    backward(1)
    to_far(1, 0)
    run(run_c, 1)
    backward(2)
    to_far(1, 1)
    backward(3)
    to_far(1, 2)
    run(run_c, 1)
    for n in (4, 5, 6, 7):
        backward(n)
        to_far(1, n - 1)
    to_far(1, 7)
    run(run_s, 1)
    each(finish_cot, 0, 1)
    run(run_s, 1)
    each(finish_cot, 2, 3)
    down_rows(0)
    finish_cot(4)
    down_rows(1)
    run(run_s, 1)
    each(finish_cot, 5, 6, 7)
    mh_all[dp] = mh_own[...]
    mh_copies = [start(mh_own, mh_all.at[dp], dev) for dev in dp_parts]
    down_rows(2)
    run(run_s, 1)
    down_rows(3)
    for n in range(8):
        upc_copies[n].wait_recv()
    up_rows(0)
    run(run_s, 1)
    up_rows(1)
    run(run_s, 1)
    each(up_rows, 2, 3)

    in_acc[...] = jnp.zeros((8, 16, IMG), F32)
    for p in range(8):
        in_acc[p, :, 0:PIECE] = lax.dot_general(
            selm[...], col[p * PIECE : (p + 1) * PIECE, :], (((1,), (1,)), ((), ())),
            precision=lax.Precision.HIGHEST, preferred_element_type=F32,
        )
    in_copies = []
    for i, (dx, dl) in enumerate(xl_parts):
        p_to = 2 * lax.rem(x + dx, 4) + lax.rem(l + dl, 2)
        in_copies.append(start(in_acc.at[p_to], in_recv.at[i], at(x=dx, l=dl)))
    for copy in in_copies:
        copy.wait_recv()
    total_in = in_acc[own_piece]
    for i in range(7):
        total_in = total_in + in_recv[i]
    y_in[y] = total_in
    y_in_copies = [start(y_in.at[y], y_in.at[y], at(y=dy)) for dy in y_parts]
    run(run_s)

    out_total = jnp.zeros((16, PIECE), F32)
    for j in both:
        prod = gc[2 * y + j, own_rows].astype(F32) * fb[j].astype(F32)
        out_total = out_total + dot_t(sel[2 * y + j, 0], prod.astype(BF16))
    y_out[y] = jnp.zeros((16, IMG), F32)
    y_out[y, :, 0:PIECE] = out_total
    y_out_copies = [start(y_out.at[y], y_out.at[y], at(y=dy)) for dy in y_parts]
    for copy in y_in_copies + y_out_copies:
        copy.wait_recv()
    s_send[0] = (y_in[0] + y_in[1]) + (y_in[2] + y_in[3])
    s_send[1] = (y_out[0] + y_out[1]) + (y_out[2] + y_out[3])
    last = start_swap(s_send, s_recv)
    for copy in mh_copies:
        copy.wait_recv()
    fin_mid[...] = jnp.concatenate([mh_all[0, 0:4, 0:HALF], mh_all[1, 0:4, 0:HALF]], axis=1)
    fin_hid[...] = jnp.concatenate([mh_all[0, 16:20, 0:HALF], mh_all[1, 16:20, 0:HALF]], axis=1)
    for j in both:
        finals[j].wait_recv()
        factor = dot(own_col[...], sel[2 * dp + j, 1])
        lo[:, lanes[j]] = (
            tok[:, lanes[j]].astype(F32) + bo_in[j].astype(F32) * factor
        ).astype(BF16)
    last.wait_recv()
    fin_in[...] = s_recv[0, 0:4, 0:PIECE] / in_fast[...].astype(F32)
    fin_out[...] = s_recv[1, 0:4, 0:PIECE]
    drain(sends)


def widen(ug, dg, lo, *small):
    def copy(*refs):
        n = len(refs) // 2
        for src, dst in zip(refs[:n], refs[n:]):
            dst[...] = src[...].astype(dst.dtype)

    def spec(a, split):
        if split:
            return pl.BlockSpec((a.shape[0] // 2, a.shape[1]), lambda i: (i, 0))
        return pl.BlockSpec(a.shape, lambda i: (0, 0))

    arrays = (ug, dg, lo) + small
    specs = [spec(a, n < 3) for n, a in enumerate(arrays)]
    return pl.pallas_call(
        copy,
        grid=(2,),
        in_specs=specs,
        out_specs=specs,
        out_shape=[
            jax.ShapeDtypeStruct(a.shape, F32 if n < 2 else a.dtype)
            for n, a in enumerate(arrays)
        ],
    )(*arrays)


def exchange(*arrays):
    vmem = pl.BlockSpec(memory_space=pltpu.VMEM)
    smem = pl.BlockSpec(memory_space=pltpu.SMEM)
    out_shape = [
        jax.ShapeDtypeStruct((PIECE, 2 * IMG), BF16),
        jax.ShapeDtypeStruct((D_BLK, FFB), BF16),
        jax.ShapeDtypeStruct((D_BLK, FFB), BF16),
        jax.ShapeDtypeStruct((4, PIECE), F32),
        jax.ShapeDtypeStruct((4, PIECE), F32),
        jax.ShapeDtypeStruct((4, FFB), F32),
        jax.ShapeDtypeStruct((4, FFB), F32),
    ]
    scratch = [
        ((N_IMG, D_BLK, IMG), BF16),
        ((N_IMG, D_BLK, IMG), BF16),
        ((N_IMG, D_BLK, IMG), BF16),
        ((N_IMG, D_BLK, IMG), BF16),
        ((FFB, FFB), BF16),
        ((16, FFB), F32),
        ((16, IMG), BF16),
        ((FFB, 16), BF16),
        ((8, 16, IMG), BF16),
        ((D_BLK, 16), BF16),
        ((PIECE, 16), BF16),
        ((N_IMG, 2, 16, IMG), BF16),
        ((16, 128), F32),
        ((2, 8, IMG), F32),
        ((7, 2, 8, IMG), F32),
        ((4, 2, 8, IMG), F32),
        ((N_IMG, 8, IMG), F32),
        ((D_BLK, 128), F32),
        ((2, N_IMG, HALF, IMG), F32),
        ((2, N_IMG, HALF, IMG), BF16),
        ((2, N_IMG, HALF, IMG), BF16),
        ((2, N_IMG, HALF, IMG), BF16),
        ((2, N_IMG, HALF, IMG), BF16),
        ((N_IMG, FFB, IMG), BF16),
        ((N_IMG, FFB, IMG), BF16),
        ((2, 2, 2, PAIR, IMG), BF16),
        ((2, 2, 4, PAIR, IMG), BF16),
        ((2, 2, PIECE, IMG), BF16),
        ((2, 2, PAIR, IMG), BF16),
        ((2, PIECE, IMG), BF16),
        ((2, PIECE, IMG), BF16),
        ((2, PIECE, IMG), BF16),
        ((8, 16, IMG), F32),
        ((7, 16, IMG), F32),
        ((4, 16, IMG), F32),
        ((4, 16, IMG), F32),
        ((2, 16, IMG), F32),
        ((2, 16, IMG), F32),
        ((32, IMG), F32),
        ((4, 32, IMG), F32),
    ]
    return pl.pallas_call(
        kernel,
        out_shape=out_shape,
        in_specs=[vmem, vmem, smem] + [vmem] * 6,
        out_specs=[vmem] * 7,
        scratch_shapes=[pltpu.VMEM(s, d) for s, d in scratch]
        + [pltpu.SemaphoreType.DMA((N_SEM,)), pltpu.SemaphoreType.DMA((N_SEM,))],
        compiler_params=pltpu.CompilerParams(
            collective_id=0, has_side_effects=True, vmem_limit_bytes=62 * 1024 * 1024
        ),
        cost_estimate=pl.CostEstimate(
            flops=14_500_000_000, bytes_accessed=12_000_000, transcendentals=1_600_000
        ),
    )(*arrays)


def body(
    tokens, member, up_weight, down_weight, in_fast, hidden_fast, mid_fast, out_fast, cotangent
):
    lo, ug, dg, in_grad, out_grad, mid_grad, hidden_grad = exchange(
        tokens.T, cotangent.T, member, in_fast, out_fast, hidden_fast, mid_fast,
        up_weight, down_weight,
    )
    ug, dg, lo, in_grad, out_grad, mid_grad, hidden_grad = widen(
        ug, dg, lo, in_grad, out_grad, mid_grad, hidden_grad
    )
    return (lo.T, ug, dg, in_grad, hidden_grad, mid_grad, out_grad)


def solution(mesh):
    grid = Mesh(mesh.devices.reshape([SIZES[a] for a in AXES]), AXES)
    dp, mp = ("h", "c"), ("y", "x", "l")
    in_specs = (
        P(dp, mp),
        P(dp),
        P(dp, mp),
        P(dp, mp),
        P(None, mp),
        P(None, mp),
        P(None, mp),
        P(None, mp),
        P(dp, mp),
    )
    out_specs = (
        P(dp, mp),
        P(dp, mp),
        P(dp, mp),
        P(None, mp),
        P(None, mp),
        P(None, mp),
        P(None, mp),
    )
    return jax.shard_map(body, mesh=grid, in_specs=in_specs, out_specs=out_specs, check_vma=False)
```
